256 devices in a mesh: seq: 128 (over x_hi, y, z, core), head: 2 (over x_lo).
Axes of the slice: x: 4 (x_hi: 2, x_lo: 2; x = x_hi * 2 + x_lo), y: 4, z: 8, core: 2. Of those that a mesh axis runs over, the one named last changes fastest.
Arguments:
- queries: bfloat16 [65536, 768], P('seq', 'head'), may hold values from -6 to 6
- keys: bfloat16 [65536, 768], P('seq', 'head'), may hold values from -6 to 6
- values: bfloat16 [65536, 768], P('seq', 'head'), may hold values from -6 to 6
- weight_out: bfloat16 [768, 768], P('head'), may hold values from -0.21875 to 0.21875
- cotangent: bfloat16 [65536, 768], P('seq', 'head'), may hold values from -6 to 6
Outputs:
- mixed: bfloat16 [65536, 768], P('seq', 'head')
- query_grad: bfloat16 [65536, 768], P('seq', 'head')
- key_grad: bfloat16 [65536, 768], P('seq', 'head')
- value_grad: bfloat16 [65536, 768], P('seq', 'head')
The draws below stay inside these ranges and needn't reach their ends.
All inputs are finite; a program needn't handle non-finite values.
Results may differ from the reference program's by a relative error of at most 0.034.
Values may be sent and summed in bfloat16 or wider, within the bound.
No kernel may reach another device: no remote copies, remote signals or barrier semaphores. Data moves between devices by JAX's collectives and lax.ppermute only.
A program may use at most 128 MiB of HBM per device.

```python
import jax
import jax.numpy as jnp
from jax import lax

HEADS = 12
HEAD_DIM = 64
WIDTH = 768
TOK_DEV = 512
TOKENS = 65536
N_SEQ = 128


def draw_queries(key, part):
    key = jax.random.fold_in(key, 11)
    return jnp.clip(jax.random.normal(key, (TOKENS, HEADS * HEAD_DIM), jnp.float32), -5.0, 5.0).astype(jnp.bfloat16)


def draw_keys(key, part):
    key = jax.random.fold_in(key, 12)
    return jnp.clip(jax.random.normal(key, (TOKENS, HEADS * HEAD_DIM), jnp.float32), -5.0, 5.0).astype(jnp.bfloat16)


def shard_levels(key, extent, cuts, smallest, top_value):
    def one(position, blocks):
        draws = jax.random.uniform(jax.random.fold_in(jax.random.fold_in(key, 6), position), (blocks,), jnp.float32, smallest / len(cuts), top_value / len(cuts))
        return jnp.repeat(jnp.exp(draws), extent[position] // blocks).reshape((-1,) + (1,) * (len(extent) - position - 1))

    gain = one(*cuts[0])
    for cut in cuts[1:]:
        gain = gain * one(*cut)
    return gain


def bell_draw(stream_key, dims, spread, reach, pieces=(), held_as=jnp.bfloat16):
    array = jax.random.normal(stream_key, dims, jnp.float32) * spread
    if len(pieces) > 0:
        array = shard_levels(stream_key, dims, pieces, -0.22, 0.18) * array
    return jnp.clip(array, min=-reach, max=reach).astype(held_as)


def setup_inputs(seed: int = 0) -> dict:
    streams_of = jax.random.split(jax.random.key(seed), 6)
    return {
        "queries": draw_queries(jax.random.fold_in(streams_of[5], 71), 0),
        "keys": draw_keys(jax.random.fold_in(streams_of[5], 71), 0),
        "values": bell_draw(streams_of[2], (TOKENS, WIDTH), 1.0, 6.0, ((0, 128), (1, 2))),
        "weight_out": bell_draw(streams_of[3], (WIDTH, WIDTH), WIDTH ** -0.5, 0.21875, ((0, 2),)),
        "cotangent": bell_draw(streams_of[4], (TOKENS, WIDTH), 1.0, 6.0, ((0, 128), (1, 2))),
    }


NEG_FILL = -1.0e30


def pick_rows(source, group_size, offsets):
    row_count = source.shape[0]
    shaped = source.reshape(row_count // group_size, group_size, source.shape[1], source.shape[2])
    chosen = jnp.arange(group_size, dtype=jnp.int32)[:, None] == offsets[None, :]
    masked = jnp.where(chosen[None, :, :, None], shaped, jnp.zeros((), source.dtype))
    return jnp.sum(masked, axis=1).astype(source.dtype)


def spread_rows(source, group_size, offsets, filler):
    chosen = jnp.arange(group_size, dtype=jnp.int32)[:, None] == offsets[None, :]
    widened = jnp.where(chosen[None, :, :, None], source[:, None], jnp.asarray(filler, source.dtype))
    return widened.reshape(source.shape[0] * group_size, source.shape[1], source.shape[2])


def settle(tensor):
    return lax.optimization_barrier(tensor.astype(jnp.bfloat16)).astype(jnp.float32)


def level_scores(query_rows, key_rows):
    return (HEAD_DIM ** -0.5) * jnp.einsum("qhd,khd->hqk", query_rows.astype(jnp.float32), key_rows.astype(jnp.float32))


def level_forward(query_rows, key_rows, value_rows):
    scores = level_scores(query_rows, key_rows)
    maxima = jnp.max(scores, axis=2)
    powers = jnp.exp(scores - maxima[:, :, None])
    totals = jnp.sum(powers, axis=2)
    weighted = jnp.einsum("hqk,khd->qhd", settle(powers), value_rows.astype(jnp.float32))
    return maxima.T, totals.T, weighted


def level_grads(query_rows, key_rows, value_rows, grad_rows, total_rows, delta_rows):
    scale_factor = HEAD_DIM ** -0.5
    probability = jnp.exp(level_scores(query_rows, key_rows) - total_rows.T[:, :, None])
    value_part = jnp.einsum("hqk,qhd->khd", settle(probability), grad_rows.astype(jnp.float32))
    prob_grad = jnp.einsum("qhd,khd->hqk", grad_rows.astype(jnp.float32), value_rows.astype(jnp.float32))
    score_grad = settle(probability * (prob_grad - delta_rows.T[:, :, None]))
    query_part = scale_factor * jnp.einsum("hqk,khd->qhd", score_grad, key_rows.astype(jnp.float32))
    key_part = scale_factor * jnp.einsum("hqk,qhd->khd", score_grad, query_rows.astype(jnp.float32))
    return query_part, key_part, value_part


def reference(queries, keys, values, weight_out, cotangent):
    head_ids = jnp.arange(HEADS, dtype=jnp.int32)
    group_sizes = (min(8, N_SEQ // 4), min(32, N_SEQ // 2), N_SEQ)
    query_all = queries.reshape(TOKENS, HEADS, HEAD_DIM)
    key_all = keys.reshape(TOKENS, HEADS, HEAD_DIM)
    value_all = values.reshape(TOKENS, HEADS, HEAD_DIM)
    level_sets = []
    for group_size in group_sizes:
        offsets = head_ids % group_size
        segments = TOKENS // (group_size * TOK_DEV)
        level_sets.append(tuple(pick_rows(member, group_size, offsets).reshape(segments, TOK_DEV, HEADS, HEAD_DIM) for member in (query_all, key_all, value_all)))

    def block_step(carried, block_no):
        first_row = block_no * TOK_DEV
        query_blk = lax.dynamic_slice_in_dim(query_all, first_row, TOK_DEV, 0)
        key_blk = lax.dynamic_slice_in_dim(key_all, first_row, TOK_DEV, 0)
        value_blk = lax.dynamic_slice_in_dim(value_all, first_row, TOK_DEV, 0)
        grad_blk = lax.dynamic_slice_in_dim(cotangent, first_row, TOK_DEV, 0)
        maxima, totals, weighted = level_forward(query_blk, key_blk, value_blk)
        max_list, total_list, weighted_list = [maxima], [totals], [weighted]
        level_parts = []
        for level_no in range(3):
            group_size = group_sizes[level_no]
            offsets = head_ids % group_size
            part_rows = TOK_DEV // group_size
            segment = block_no // group_size
            query_set, key_set, value_set = level_sets[level_no]
            key_group = lax.dynamic_index_in_dim(key_set, segment, 0, keepdims=False)
            value_group = lax.dynamic_index_in_dim(value_set, segment, 0, keepdims=False)
            query_group = lax.dynamic_index_in_dim(query_set, segment, 0, keepdims=False)
            query_part = lax.dynamic_slice_in_dim(query_group, (block_no % group_size) * part_rows, part_rows, 0)
            maxima, totals, weighted = level_forward(query_part, key_group, value_group)
            max_list.append(spread_rows(maxima[:, :, None], group_size, offsets, NEG_FILL)[:, :, 0])
            total_list.append(spread_rows(totals[:, :, None], group_size, offsets, 0.0)[:, :, 0])
            weighted_list.append(spread_rows(weighted, group_size, offsets, 0.0))
            level_parts.append((group_size, offsets, segment, query_part, key_group, value_group))
        peak_score = max_list[0]
        for level_max in max_list[1:]:
            peak_score = jnp.maximum(peak_score, level_max)
        denominator = jnp.zeros(peak_score.shape, jnp.float32)
        for level_max, level_total in zip(max_list, total_list):
            denominator = denominator + jnp.exp(level_max - peak_score) * level_total
        log_total = peak_score + jnp.log(denominator)
        attended = jnp.zeros(weighted_list[0].shape, jnp.float32)
        for level_max, level_weighted in zip(max_list, weighted_list):
            attended = attended + jnp.exp(level_max - log_total)[:, :, None] * level_weighted
        attended = attended.astype(jnp.bfloat16)
        mixed_blk = jnp.dot(attended.reshape(TOK_DEV, WIDTH), weight_out, preferred_element_type=jnp.float32).astype(jnp.bfloat16)
        out_grad = jnp.dot(grad_blk, weight_out.T, preferred_element_type=jnp.float32).astype(jnp.bfloat16).reshape(TOK_DEV, HEADS, HEAD_DIM)
        row_delta = jnp.sum(out_grad.astype(jnp.float32) * attended.astype(jnp.float32), axis=2)
        query_total, key_local, value_local = level_grads(query_blk, key_blk, value_blk, out_grad, log_total, row_delta)
        new_carried = []
        for level_no in range(3):
            group_size, offsets, segment, query_part, key_group, value_group = level_parts[level_no]
            grad_part = pick_rows(out_grad, group_size, offsets)
            total_part = pick_rows(log_total[:, :, None], group_size, offsets)[:, :, 0]
            delta_part = pick_rows(row_delta[:, :, None], group_size, offsets)[:, :, 0]
            query_piece, key_terms, value_terms = level_grads(query_part, key_group, value_group, grad_part, total_part, delta_part)
            query_total = query_total + spread_rows(query_piece, group_size, offsets, 0.0)
            key_acc, value_acc = carried[level_no]
            new_carried.append((key_acc.at[segment].add(key_terms), value_acc.at[segment].add(value_terms)))
        return tuple(new_carried), (mixed_blk, query_total.astype(jnp.bfloat16), key_local, value_local)

    carry_init = tuple((jnp.zeros((TOKENS // (group_size * TOK_DEV), TOK_DEV, HEADS, HEAD_DIM), jnp.float32), jnp.zeros((TOKENS // (group_size * TOK_DEV), TOK_DEV, HEADS, HEAD_DIM), jnp.float32)) for group_size in group_sizes)
    final_carried, outputs = lax.scan(block_step, carry_init, jnp.arange(TOKENS // TOK_DEV, dtype=jnp.int32))
    mixed_all, query_all_grad, key_local, value_local = outputs
    key_total = key_local.reshape(TOKENS, HEADS, HEAD_DIM)
    value_total = value_local.reshape(TOKENS, HEADS, HEAD_DIM)
    for level_no in range(3):
        group_size = group_sizes[level_no]
        offsets = head_ids % group_size
        key_acc, value_acc = final_carried[level_no]
        key_total = key_total + spread_rows(key_acc.reshape(-1, HEADS, HEAD_DIM), group_size, offsets, 0.0)
        value_total = value_total + spread_rows(value_acc.reshape(-1, HEADS, HEAD_DIM), group_size, offsets, 0.0)
    return (mixed_all.reshape(TOKENS, WIDTH), query_all_grad.reshape(TOKENS, WIDTH), key_total.reshape(TOKENS, WIDTH).astype(jnp.bfloat16), value_total.reshape(TOKENS, WIDTH).astype(jnp.bfloat16))
```

```python
import functools

import jax
import jax.numpy as jnp
import numpy as np
from jax import lax
from jax.experimental import pallas as pl
from jax.experimental.pallas import tpu as pltpu
from jax.sharding import PartitionSpec as P

HEAD_DIM = 64
LOCAL_HEADS = 6
ROWS = 512
KEPT = 64
SCALE = HEAD_DIM ** -0.5
BF = jnp.bfloat16
F32 = jnp.float32
MASKED = 1e30


def kept_rows(head):
    phase = head // 8
    third = [16 * i + phase for i in range(4)]
    second = [4 * i + phase for i in range(16) if i % 4]
    first = [i for i in range(64) if i % 4 != phase]
    return [8 * i + head % 8 for i in third + second + first]


def one_hot_tables():
    table = np.zeros((2, LOCAL_HEADS * KEPT, ROWS), np.float32)
    for half in range(2):
        for local in range(LOCAL_HEADS):
            for place, row in enumerate(kept_rows(half * LOCAL_HEADS + local)):
                table[half, local * KEPT + place, row] = 1.0
    return table


def subset_table(groups, wide, narrow):
    table = np.zeros((groups * narrow, groups * wide), np.float32)
    for group in range(groups):
        for place in range(narrow):
            table[group * narrow + place, group * wide + place] = 1.0
    return table


def dot_nn(left, right):
    return lax.dot_general(left, right, (((1,), (0,)), ((), ())), preferred_element_type=F32)


def dot_nt(left, right):
    return lax.dot_general(left, right, (((1,), (1,)), ((), ())), preferred_element_type=F32)


def dot_tn(left, right):
    return lax.dot_general(left, right, (((0,), (0,)), ((), ())), preferred_element_type=F32)


def split2(value):
    high = value.astype(BF)
    return high, (value - high.astype(F32)).astype(BF)


def split3(value):
    high = value.astype(BF)
    rest = value - high.astype(F32)
    middle = rest.astype(BF)
    return high, middle, (rest - middle.astype(F32)).astype(BF)


def stat_block(log_row, delta_row):
    pieces = split3(log_row) + split3(delta_row)
    rows = [piece.astype(F32) for piece in pieces]
    zero = jnp.zeros_like(log_row)
    return jnp.concatenate(rows + [zero, zero], axis=0)


def stat_rows(block):
    block = block.astype(F32)
    log_row = block[0:1] + block[1:2] + block[2:3]
    delta_row = block[3:4] + block[4:5] + block[5:6]
    return log_row, delta_row


def head_cols(ref, head):
    return ref[:, head * HEAD_DIM:(head + 1) * HEAD_DIM]


def log_add(first, second):
    peak = jnp.maximum(first, second)
    return peak + jnp.log(jnp.exp(first - peak) + jnp.exp(second - peak))


def local_forward(q_ref, k_ref, v_ref, out_t_ref, log_ref):
    for head in range(LOCAL_HEADS):
        query = head_cols(q_ref, head) * BF(SCALE)
        scores = dot_nt(head_cols(k_ref, head), query)
        peak = jnp.max(scores, axis=0, keepdims=True)
        powers = jnp.exp(scores - peak)
        total = jnp.sum(powers, axis=0, keepdims=True)
        weighted = dot_tn(head_cols(v_ref, head), powers.astype(BF))
        out_t_ref[head * HEAD_DIM:(head + 1) * HEAD_DIM, :] = weighted / total
        log_ref[head:head + 1, :] = peak + jnp.log(total)
    log_ref[LOCAL_HEADS:, :] = jnp.zeros((8 - LOCAL_HEADS, ROWS), F32)


def pack_rows(q_ref, k_ref, v_ref, own_cot_ref, other_cot_ref, own_w_ref, other_w_ref, hot_ref, out_t_ref, log_ref,
              grad_ref, delta_ref, payload_ref):
    grad = dot_nt(own_cot_ref[...], own_w_ref[...]) + dot_nt(other_cot_ref[...], other_w_ref[...])
    grad_ref[...] = grad.astype(BF)
    grad_t = dot_nt(own_w_ref[...], own_cot_ref[...]) + dot_nt(other_w_ref[...], other_cot_ref[...])
    product = grad_t.astype(BF).astype(F32) * out_t_ref[...]
    delta_ref[LOCAL_HEADS:, :] = jnp.zeros((8 - LOCAL_HEADS, ROWS), F32)
    for head in range(LOCAL_HEADS):
        hot = hot_ref[head * KEPT:(head + 1) * KEPT, :]
        delta = jnp.sum(product[head * HEAD_DIM:(head + 1) * HEAD_DIM], axis=0, keepdims=True)
        delta_ref[head:head + 1, :] = delta
        joined = jnp.concatenate(
            [head_cols(ref, head) for ref in (q_ref, k_ref, v_ref, grad_ref)], axis=1
        )
        payload_ref[head, :KEPT, :] = dot_nn(hot, joined).astype(BF)
        stats = stat_block(log_ref[head:head + 1, :], delta).astype(BF)
        payload_ref[head, KEPT:, :] = widen_stats(dot_nt(stats, hot))
    for spare in range(LOCAL_HEADS, 8):
        payload_ref[spare] = jnp.zeros((KEPT + 16, 256), BF)


def widen_stats(block):
    wide = jnp.concatenate([block, jnp.zeros((8, 256 - block.shape[1]), F32)], axis=1)
    return jnp.concatenate([wide, jnp.zeros((8, 256), F32)], axis=0).astype(BF)


def local_backward(q_ref, k_ref, v_ref, grad_ref, log_ref, delta_ref, kept_ref, out_t_ref,
                   dq_ref, dk_ref, dv_ref, att_t_ref):
    dq_t = []
    for head in range(LOCAL_HEADS):
        span = slice(head * HEAD_DIM, (head + 1) * HEAD_DIM)
        query = head_cols(q_ref, head) * BF(SCALE)
        key = head_cols(k_ref, head)
        grad = head_cols(grad_ref, head)
        kept = kept_ref[head:head + 1, :]
        probability = jnp.exp(dot_nt(key, query) - (log_ref[head:head + 1, :] + kept * MASKED))
        score_grad = probability * (dot_nt(head_cols(v_ref, head), grad) - delta_ref[head:head + 1, :])
        score_grad = score_grad.astype(BF)
        dv_ref[:, span] = dot_nn(probability.astype(BF), grad)
        dk_ref[:, span] = dot_nn(score_grad, query)
        dq_t.append(dot_tn(key, score_grad))
        att_t_ref[span, :] = (out_t_ref[span, :] * (1.0 - kept)).astype(BF)
    dq_ref[...] = jnp.concatenate(dq_t, axis=0).T * SCALE


def set_stats(query, key, value, grad):
    scores = dot_nt(key, query)
    peak = jnp.max(scores, axis=0, keepdims=True)
    powers = jnp.exp(scores - peak)
    total = jnp.sum(powers, axis=0, keepdims=True)
    prob_grad = dot_nt(value, grad)
    delta = jnp.sum(powers * prob_grad, axis=0, keepdims=True) / total
    return powers, total, peak + jnp.log(total), delta


def merge(old_log, old_delta, new_log, new_delta):
    joint = log_add(old_log, new_log)
    return joint, jnp.exp(old_log - joint) * old_delta + jnp.exp(new_log - joint) * new_delta


def split_cols(data):
    return (data[:, :64] * BF(SCALE), data[:, 64:128], data[:, 128:192], data[:, 192:])


def first_data(block_ref):
    return block_ref[:, :KEPT, :].reshape(ROWS, 256)


def gathered(block_ref):
    data = block_ref[:, :128, :].reshape(ROWS, 256)
    stats = jnp.concatenate([block_ref[i, 128:136, :128].astype(F32) for i in range(4)], axis=1)
    return data, stats


def level_one(block_ref, pick_ref, payload_ref, stat_ref, out_t_ref):
    data = first_data(block_ref)
    query, key, value, grad = split_cols(data)
    stats = jnp.concatenate([block_ref[i, KEPT:KEPT + 8, :KEPT].astype(F32) for i in range(8)], axis=1)
    old_log, old_delta = stat_rows(stats)
    powers, total, new_log, new_delta = set_stats(query, key, value, grad)
    joint, delta = merge(old_log, old_delta, new_log, new_delta)
    out_t_ref[...] = dot_tn(value, powers.astype(BF)) * (jnp.exp(new_log - joint) / total)
    stat_ref[0:1, :] = joint
    stat_ref[1:2, :] = delta
    stat_ref[2:, :] = jnp.zeros((6, ROWS), F32)
    payload_ref[:128, :] = block_ref[:, :16, :].reshape(128, 256)
    picked = dot_nt(stat_block(joint, delta).astype(BF), pick_ref[...])
    payload_ref[128:, :] = widen_stats(picked)


def level_two(block_ref, pick_ref, payload_ref, stat_ref, out_t_ref):
    data, stats = gathered(block_ref)
    query, key, value, grad = split_cols(data)
    old_log, old_delta = stat_rows(stats)
    powers, total, new_log, new_delta = set_stats(query, key, value, grad)
    joint, delta = merge(old_log, old_delta, new_log, new_delta)
    weight = (jnp.exp(new_log - joint) / total)[:, :128]
    out_t_ref[...] = dot_tn(value, powers[:, :128].astype(BF)) * weight
    stat_ref[0:1, :] = joint
    stat_ref[1:2, :] = delta
    stat_ref[2:, :] = jnp.zeros((6, ROWS), F32)
    payload_ref[:128, :] = dot_nn(pick_ref[...], data).astype(BF)
    picked = dot_nt(stat_block(joint, delta).astype(BF), pick_ref[...])
    payload_ref[128:, :] = widen_stats(picked)


def set_grads(data, log_row, delta_row, own):
    query, key, value, grad = split_cols(data)
    probability = jnp.exp(dot_nt(key, query) - log_row)
    score_grad = (probability * (dot_nt(value, grad) - delta_row)).astype(BF)
    key_grad = dot_nn(score_grad[:own], query)
    value_grad = dot_nn(probability[:own].astype(BF), grad)
    query_grad_t = dot_tn(key, score_grad[:, :own]) * SCALE
    return query_grad_t, jnp.concatenate([key_grad, value_grad], axis=1)


def spread_lanes(value, pick):
    high, low = split2(value)
    return dot_nn(high, pick) + dot_nn(low, pick)


def spread_stats(log_row, delta_row, pick):
    return stat_rows(dot_nn(stat_block(log_row, delta_row).astype(BF), pick))


def level_three(first_ref, second_ref, third_ref, stat1_ref, stat2_ref, out1_ref, out2_ref, pick2_ref, pick3_ref,
                payload_ref):
    pick2 = pick2_ref[...]
    pick3 = pick3_ref[...]
    in_second = jnp.sum(pick2.astype(F32), axis=0, keepdims=True) > 0.5
    in_third = jnp.sum(pick3.astype(F32), axis=0, keepdims=True) > 0.5

    data3, stats3 = gathered(third_ref)
    query, key, value, grad = split_cols(data3)
    old_log, old_delta = stat_rows(stats3)
    powers, total, new_log, new_delta = set_stats(query, key, value, grad)
    log3, delta3 = merge(old_log, old_delta, new_log, new_delta)
    weight = (jnp.exp(new_log - log3) / total)[:, :128]
    out3 = dot_tn(value, powers[:, :128].astype(BF)) * weight
    dq3, dkv3 = set_grads(data3, log3, delta3, 128)

    spread_log, spread_delta = spread_stats(log3[:, :128], delta3[:, :128], pick3)
    log2 = jnp.where(in_third, spread_log, stat2_ref[0:1, :])
    delta2 = jnp.where(in_third, spread_delta, stat2_ref[1:2, :])
    data2, _ = gathered(second_ref)
    dq2, dkv2 = set_grads(data2, log2, delta2, 128)
    own3 = pick3[:32, :128]
    own_lane = lax.broadcasted_iota(jnp.int32, (1, 128), 1) < 32
    merged_t = jnp.concatenate([dq3, out3], axis=0)
    merged_t = jnp.where(own_lane, merged_t, 0.0)
    own_pick = jnp.concatenate([own3, jnp.zeros((96, 128), BF)], axis=0)
    fade2 = jnp.exp(stat2_ref[0:1, :128] - log2[:, :128])
    base_t = jnp.concatenate([dq2, out2_ref[...] * fade2], axis=0)
    merged_t = base_t + spread_lanes(merged_t, own_pick)
    high, low = split2(dkv3[:32])
    dkv2 = dkv2 + dot_tn(own3, high) + dot_tn(own3, low)

    spread_log, spread_delta = spread_stats(log2[:, :128], delta2[:, :128], pick2)
    log1 = jnp.where(in_second, spread_log, stat1_ref[0:1, :])
    delta1 = jnp.where(in_second, spread_delta, stat1_ref[1:2, :])
    data1 = first_data(first_ref)
    dq1, dkv1 = set_grads(data1, log1, delta1, ROWS)
    fade1 = jnp.exp(stat1_ref[0:1, :] - log1)
    base_t = jnp.concatenate([dq1, out1_ref[...] * fade1], axis=0)
    merged_t = base_t + spread_lanes(merged_t, pick2)
    high, low = split2(dkv2)
    dkv1 = dkv1 + dot_tn(pick2, high) + dot_tn(pick2, low)

    rows = jnp.concatenate([merged_t.T, dkv1], axis=1).astype(BF)
    payload_ref[:, :KEPT, :] = rows.reshape(8, KEPT, 256)
    stats = stat_block(log1, delta1)
    for owner in range(8):
        payload_ref[owner, KEPT:, :] = widen_stats(stats[:, owner * KEPT:(owner + 1) * KEPT])


def kept_attended(back_ref, hot_ref, out_t_ref, log_ref, att_ref):
    for head in range(LOCAL_HEADS):
        span = slice(head * HEAD_DIM, (head + 1) * HEAD_DIM)
        hot = hot_ref[head * KEPT:(head + 1) * KEPT, :]
        high, low = split2(out_t_ref[span, :])
        local = dot_nt(high, hot) + dot_nt(low, hot)
        zero = jnp.zeros((1, ROWS), F32)
        local_log, _ = stat_rows(dot_nt(stat_block(log_ref[head:head + 1, :], zero).astype(BF), hot))
        log_total, _ = stat_rows(back_ref[head, KEPT:KEPT + 8, :KEPT])
        sparse = back_ref[head, :KEPT, 64:128].astype(F32).T
        att_ref[span, :] = (local * jnp.exp(local_log - log_total) + sparse).astype(BF)


def final_grads(q_ref, k_ref, v_ref, sent_ref, back_ref, tall_ref, dq_ref, dk_ref, dv_ref,
                dq_out_ref, dk_out_ref, dv_out_ref):
    for head in range(LOCAL_HEADS):
        span = slice(head * HEAD_DIM, (head + 1) * HEAD_DIM)
        key = head_cols(k_ref, head)
        query = sent_ref[head, :KEPT, :64] * BF(SCALE)
        grad = sent_ref[head, :KEPT, 192:]
        tall = head_cols(tall_ref, head)
        log_total, delta = stat_rows(back_ref[head, KEPT:KEPT + 8, :KEPT])
        probability = jnp.exp(dot_nt(key, query) - log_total)
        score_grad = (probability * (dot_nt(head_cols(v_ref, head), grad) - delta)).astype(BF)
        back = back_ref[head, :KEPT, :]
        dk_more = dot_nn(
            jnp.concatenate([score_grad, tall], axis=1), jnp.concatenate([query, back[:, 128:192]], axis=0)
        )
        dv_more = dot_nn(
            jnp.concatenate([probability.astype(BF), tall], axis=1),
            jnp.concatenate([grad, back[:, 192:]], axis=0),
        )
        high, low = split2(dot_tn(score_grad, key) * SCALE + back[:, :64].astype(F32))
        dq_more = dot_nn(jnp.concatenate([tall, tall], axis=1), jnp.concatenate([high, low], axis=0))
        dq_out_ref[:, span] = (dq_ref[:, span] + dq_more).astype(BF)
        dk_out_ref[:, span] = (dk_ref[:, span] + dk_more).astype(BF)
        dv_out_ref[:, span] = (dv_ref[:, span] + dv_more).astype(BF)


def mix_rows(own_att_ref, other_att_ref, own_kept_ref, other_kept_ref, own_hot_ref, other_hot_ref,
             own_w_ref, other_w_ref, mixed_ref):
    total = jnp.zeros((ROWS, 384), F32)
    for att_ref, kept_ref, hot_ref, w_ref in (
        (own_att_ref, own_kept_ref, own_hot_ref, own_w_ref),
        (other_att_ref, other_kept_ref, other_hot_ref, other_w_ref),
    ):
        parts = []
        for head in range(LOCAL_HEADS):
            span = slice(head * HEAD_DIM, (head + 1) * HEAD_DIM)
            hot = hot_ref[head * KEPT:(head + 1) * KEPT, :]
            parts.append((att_ref[span, :].astype(F32) + dot_nn(kept_ref[span, :], hot)).astype(BF))
        total = total + dot_tn(jnp.concatenate(parts, axis=0), w_ref[...])
    mixed_ref[...] = total.astype(BF)


def call(kernel, outs, *args, flops=0):
    shapes = tuple(jax.ShapeDtypeStruct(shape, dtype) for shape, dtype in outs)
    moved = sum(a.size * a.dtype.itemsize for a in args) + sum(
        int(np.prod(shape)) * jnp.dtype(dtype).itemsize for shape, dtype in outs
    )
    result = pl.pallas_call(
        kernel,
        out_shape=shapes,
        in_specs=[pl.BlockSpec(memory_space=pltpu.VMEM)] * len(args),
        out_specs=tuple(pl.BlockSpec(memory_space=pltpu.VMEM) for _ in outs),
        compiler_params=pltpu.CompilerParams(vmem_limit_bytes=40 * 1024 * 1024),
        cost_estimate=pl.CostEstimate(flops=flops, bytes_accessed=moved, transcendentals=0),
        name=kernel.__name__,
    )(*args)
    return result


def partner(array):
    return lax.ppermute(array, "head", [(0, 1), (1, 0)])


def flip(array, bit):
    return lax.ppermute(array, "seq", [(i, i ^ 1 << bit) for i in range(lax.axis_size("seq"))])


def body(queries, keys, values, weight_out, cotangent):
    seq_count = lax.axis_size("seq")
    half = lax.axis_index("head")
    octets = [[8 * i + j for j in range(8)] for i in range(seq_count // 8)]
    hots = jnp.asarray(one_hot_tables(), BF)
    own_hot = lax.dynamic_index_in_dim(hots, half, 0, keepdims=False)
    other_hot = lax.dynamic_index_in_dim(hots, 1 - half, 0, keepdims=False)
    tall = lax.dynamic_index_in_dim(jnp.asarray(np.swapaxes(one_hot_tables(), 1, 2), BF), half, 0, keepdims=False)
    pick2 = jnp.asarray(subset_table(8, 64, 16), BF)
    pick3 = jnp.asarray(subset_table(32, 16, 4), BF)
    kept_table = np.zeros((2, 8, ROWS), np.float32)
    for head in range(2 * LOCAL_HEADS):
        kept_table[head // LOCAL_HEADS, head % LOCAL_HEADS, kept_rows(head)] = 1.0
    kept = lax.dynamic_index_in_dim(jnp.asarray(kept_table), half, 0, keepdims=False)
    own_w = lax.dynamic_slice_in_dim(weight_out, half * 384, 384, 1)
    other_w = lax.dynamic_slice_in_dim(weight_out, (1 - half) * 384, 384, 1)

    other_cot = partner(cotangent)
    out_t, log0 = call(local_forward, [((384, ROWS), F32), ((8, ROWS), F32)], queries, keys, values, flops=400000000)
    grad, delta0, sent = call(
        pack_rows,
        [((ROWS, 384), BF), ((8, ROWS), F32), ((8, KEPT + 16, 256), BF)],
        queries, keys, values, cotangent, other_cot, own_w, other_w, own_hot, out_t, log0, flops=600000000,
    )
    block1 = lax.all_to_all(sent, "seq", 0, 0, axis_index_groups=octets)
    mix_w = partner(other_w)
    dq, dk, dv, att_t = call(
        local_backward,
        [((ROWS, 384), F32), ((ROWS, 384), F32), ((ROWS, 384), F32), ((384, ROWS), BF)],
        queries, keys, values, grad, log0, delta0, kept, out_t, flops=1000000000,
    )
    other_att_t = partner(att_t)

    sent2, stat1, out1 = call(
        level_one, [((144, 256), BF), ((8, ROWS), F32), ((64, ROWS), F32)], block1, pick2, flops=100000000
    )
    block2 = jnp.stack([sent2, flip(sent2, 3)])
    block2 = jnp.concatenate([block2, flip(block2, 4)])
    sent3, stat2, out2 = call(
        level_two, [((144, 256), BF), ((8, ROWS), F32), ((64, 128), F32)], block2, pick3, flops=100000000
    )
    block3 = jnp.stack([sent3, flip(sent3, 5)])
    block3 = jnp.concatenate([block3, flip(block3, 6)])
    (returned,) = call(
        level_three, [((8, KEPT + 16, 256), BF)],
        block1, block2, block3, stat1, stat2, out1, out2, pick2, pick3, flops=300000000,
    )
    back = lax.all_to_all(returned, "seq", 0, 0, axis_index_groups=octets)
    (own_kept,) = call(kept_attended, [((384, KEPT), BF)], back, own_hot, out_t, log0, flops=50000000)
    other_kept = partner(own_kept)
    query_grad, key_grad, value_grad = call(
        final_grads, [((ROWS, 384), BF)] * 3, queries, keys, values, sent, back, tall, dq, dk, dv, flops=200000000
    )
    (mixed,) = call(
        mix_rows, [((ROWS, 384), BF)],
        att_t, other_att_t, own_kept, other_kept, own_hot, other_hot, own_w, mix_w, flops=400000000,
    )
    return mixed, query_grad, key_grad, value_grad


def solution(mesh):
    specs = P("seq", "head")
    return jax.shard_map(
        body,
        mesh=mesh,
        in_specs=(specs, specs, specs, P("head", None), specs),
        out_specs=(specs, specs, specs, specs),
        check_vma=False,
    )
```

```python
import jax
import jax.numpy as jnp
import numpy as np
from jax import lax
from jax.experimental import pallas as pl
from jax.experimental.pallas import tpu as pltpu
from jax.sharding import PartitionSpec as P

HEAD_DIM = 64
LOCAL_HEADS = 6
PAIRS = LOCAL_HEADS // 2
ROWS = 512
KEPT = 64
WIDE = 384
SCALE = HEAD_DIM ** -0.5
BF = jnp.bfloat16
F32 = jnp.float32
MASKED = 1e30
VMEM_LIMIT = 24 * 1024 * 1024


def iota(shape, axis):
    return lax.broadcasted_iota(jnp.int32, shape, axis)


def kept_row(place, head):
    phase = lax.shift_right_logical(head, 3)
    third = 16 * place + phase
    later = place - 4
    second = 4 * (later + lax.shift_right_arithmetic(later * 11, 5) + 1) + phase
    last = place - 16
    group = lax.shift_right_arithmetic(last * 171, 9)
    spot = last - 3 * group
    first = 4 * group + spot + jnp.where(spot >= phase, 1, 0)
    chosen = jnp.where(place < 4, third, jnp.where(place < 16, second, first))
    return 8 * chosen + jnp.bitwise_and(head, 7)


def one_hot(match):
    return jnp.where(match, 1.0, 0.0).astype(BF)


def flat_pick(head):
    return one_hot(iota((KEPT, ROWS), 1) == kept_row(iota((KEPT, ROWS), 0), head))


def tall_pick(head):
    return one_hot(iota((ROWS, KEPT), 0) == kept_row(iota((ROWS, KEPT), 1), head))


def subset_pick(wide, narrow):
    place = iota((128, ROWS), 0)
    group = lax.shift_right_logical(place, narrow)
    target = lax.shift_left(group, wide) + jnp.bitwise_and(place, (1 << narrow) - 1)
    return one_hot(iota((128, ROWS), 1) == target)


def dot_nn(left, right):
    return lax.dot_general(left, right, (((1,), (0,)), ((), ())), preferred_element_type=F32)


def dot_nt(left, right):
    return lax.dot_general(left, right, (((1,), (1,)), ((), ())), preferred_element_type=F32)


def dot_tn(left, right):
    return lax.dot_general(left, right, (((0,), (0,)), ((), ())), preferred_element_type=F32)


def split2(value):
    high = value.astype(BF)
    return high, (value - high.astype(F32)).astype(BF)


def split3(value):
    high = value.astype(BF)
    rest = value - high.astype(F32)
    middle = rest.astype(BF)
    return high, middle, (rest - middle.astype(F32)).astype(BF)


def stat_block(log_row, delta_row):
    pieces = split3(log_row) + split3(delta_row)
    rows = [piece.astype(F32) for piece in pieces]
    zero = jnp.zeros_like(log_row)
    return jnp.concatenate(rows + [zero, zero], axis=0)


def stat_rows(block):
    block = block.astype(F32)
    log_row = block[0:1] + block[1:2] + block[2:3]
    delta_row = block[3:4] + block[4:5] + block[5:6]
    return log_row, delta_row


def log_add(first, second):
    peak = jnp.maximum(first, second)
    return peak + jnp.log(jnp.exp(first - peak) + jnp.exp(second - peak))


def span(local):
    return slice(local * HEAD_DIM, (local + 1) * HEAD_DIM)


def cols(pair):
    return slice(pair * 128, (pair + 1) * 128)


def owner_of(info_ref, local):
    return jnp.bitwise_xor(info_ref[1], local)


def head_of(half, local):
    return half * LOCAL_HEADS + local


def local_forward(info_ref, q_ref, k_ref, v_ref, q_out_ref, k_out_ref, v_out_ref, out_t_ref, log_ref,
                  att_t_ref, kept_out_ref, kept_log_ref, sems):
    moves = []
    for pair in range(PAIRS):
        for which, (source, target) in enumerate(((q_ref, q_out_ref), (k_ref, k_out_ref), (v_ref, v_out_ref))):
            move = pltpu.make_async_copy(
                source.at[:, cols(pair)], target.at[:, cols(pair)], sems.at[pair, which]
            )
            move.start()
            moves.append(move)
    log_ref[LOCAL_HEADS:, :] = jnp.zeros((8 - LOCAL_HEADS, ROWS), F32)
    kept_log_ref[LOCAL_HEADS:, :] = jnp.zeros((8 - LOCAL_HEADS, KEPT), F32)
    for local in range(LOCAL_HEADS):
        if local % 2 == 0:
            for move in moves[local // 2 * 3:local // 2 * 3 + 3]:
                move.wait()
        scores = dot_nt(k_out_ref[:, span(local)], q_out_ref[:, span(local)] * BF(SCALE))
        peak = jnp.max(scores, axis=0, keepdims=True)
        powers = jnp.exp(scores - peak)
        total = jnp.sum(powers, axis=0, keepdims=True)
        out_t = dot_tn(v_out_ref[:, span(local)], powers.astype(BF)) / total
        log_row = peak + jnp.log(total)
        out_t_ref[span(local), :] = out_t
        log_ref[local:local + 1, :] = log_row
        head = head_of(info_ref[0], local)
        is_kept = jnp.bitwise_and(iota((1, ROWS), 1), 7) == jnp.bitwise_and(head, 7)
        att_t_ref[span(local), :] = jnp.where(is_kept, 0.0, out_t).astype(BF)
        hot = flat_pick(head)
        high, low = split2(out_t)
        kept_out_ref[:, span(local)] = dot_nt(hot, high) + dot_nt(hot, low)
        kept_log_ref[local:local + 1, :] = stat_rows(dot_nt(stat_block(log_row, log_row).astype(BF), hot))[0]


def pack_rows(info_ref, q_ref, k_ref, v_ref, own_cot_ref, other_cot_ref, w_ref, out_t_ref, log_ref,
              grad_ref, delta_ref, payload_ref):
    own_w = w_ref[:, pl.ds(pl.multiple_of(info_ref[0] * WIDE, 128), WIDE)]
    other_w = w_ref[:, pl.ds(pl.multiple_of((1 - info_ref[0]) * WIDE, 128), WIDE)]
    grad = (dot_nt(own_cot_ref[...], own_w) + dot_nt(other_cot_ref[...], other_w)).astype(BF)
    grad_ref[...] = grad
    product = grad.astype(F32).T * out_t_ref[...]
    delta_ref[LOCAL_HEADS:, :] = jnp.zeros((8 - LOCAL_HEADS, ROWS), F32)
    for local in range(LOCAL_HEADS):
        owner = owner_of(info_ref, local)
        hot = flat_pick(head_of(info_ref[0], local))
        delta = jnp.sum(product[span(local)], axis=0, keepdims=True)
        delta_ref[local:local + 1, :] = delta
        joined = jnp.concatenate([part[:, span(local)] for part in (q_ref, k_ref, v_ref, grad)], axis=1)
        rows = dot_nn(hot, joined).astype(BF)
        payload_ref[owner, :KEPT, :] = rows[:, :128]
        payload_ref[owner, KEPT:2 * KEPT, :] = rows[:, 128:]
        stats = stat_block(log_ref[local:local + 1, :], delta).astype(BF)
        payload_ref[owner, 2 * KEPT:, :] = widen_stats(dot_nt(stats, hot))
    for spare in range(LOCAL_HEADS, 8):
        payload_ref[owner_of(info_ref, spare)] = jnp.zeros((2 * KEPT + 16, 128), BF)


def widen_stats(block):
    if block.shape[1] < 128:
        block = jnp.concatenate([block, jnp.zeros((8, 128 - block.shape[1]), F32)], axis=1)
    return jnp.concatenate([block, jnp.zeros((8, 128), F32)], axis=0).astype(BF)


def local_backward(info_ref, q_ref, k_ref, v_ref, grad_ref, log_ref, delta_ref, dq_ref, dk_ref, dv_ref):
    for pair in range(PAIRS):
        dq_t, dk, dv = [], [], []
        for local in (2 * pair, 2 * pair + 1):
            query = q_ref[:, span(local)] * BF(SCALE)
            key = k_ref[:, span(local)]
            grad = grad_ref[:, span(local)]
            head = head_of(info_ref[0], local)
            is_kept = jnp.bitwise_and(iota((1, ROWS), 1), 7) == jnp.bitwise_and(head, 7)
            log_row = jnp.where(is_kept, MASKED, log_ref[local:local + 1, :])
            probability = jnp.exp(dot_nt(key, query) - log_row)
            score_grad = probability * (dot_nt(v_ref[:, span(local)], grad) - delta_ref[local:local + 1, :])
            score_grad = score_grad.astype(BF)
            dv.append(dot_nn(probability.astype(BF), grad))
            dk.append(dot_nn(score_grad, query))
            dq_t.append(dot_tn(key, score_grad))
        dq_ref[:, cols(pair)] = jnp.concatenate(dq_t, axis=0).T * SCALE
        dk_ref[:, cols(pair)] = jnp.concatenate(dk, axis=1)
        dv_ref[:, cols(pair)] = jnp.concatenate(dv, axis=1)


def set_stats(query, key, value, grad):
    scores = dot_nt(key, query)
    peak = jnp.max(scores, axis=0, keepdims=True)
    powers = jnp.exp(scores - peak)
    total = jnp.sum(powers, axis=0, keepdims=True)
    prob_grad = dot_nt(value, grad)
    delta = jnp.sum(powers * prob_grad, axis=0, keepdims=True) / total
    return powers, total, peak + jnp.log(total), delta


def merge(old_log, old_delta, new_log, new_delta):
    joint = log_add(old_log, new_log)
    return joint, jnp.exp(old_log - joint) * old_delta + jnp.exp(new_log - joint) * new_delta


def split_set(joined, other):
    return joined[:, :64] * BF(SCALE), joined[:, 64:], other[:, :64], other[:, 64:]


def first_set(block_ref):
    return split_set(
        block_ref[:, :KEPT, :].reshape(ROWS, 128), block_ref[:, KEPT:2 * KEPT, :].reshape(ROWS, 128)
    )


def later_set(block_ref):
    return split_set(block_ref[:, :128, :].reshape(ROWS, 128), block_ref[:, 128:256, :].reshape(ROWS, 128))


def later_stats(block_ref):
    return stat_rows(jnp.concatenate([block_ref[i, 256:264, :].astype(F32) for i in range(4)], axis=1))


def level_one(block_ref, payload_ref, stat_ref, out_t_ref):
    query, key, value, grad = first_set(block_ref)
    stats = jnp.concatenate([block_ref[i, 128:136, :KEPT].astype(F32) for i in range(8)], axis=1)
    old_log, old_delta = stat_rows(stats)
    powers, total, new_log, new_delta = set_stats(query, key, value, grad)
    joint, delta = merge(old_log, old_delta, new_log, new_delta)
    out_t_ref[...] = dot_tn(value, powers.astype(BF)) * (jnp.exp(new_log - joint) / total)
    stat_ref[0:1, :] = joint
    stat_ref[1:2, :] = delta
    stat_ref[2:, :] = jnp.zeros((6, ROWS), F32)
    payload_ref[:128, :] = block_ref[:, :16, :].reshape(128, 128)
    payload_ref[128:256, :] = block_ref[:, KEPT:KEPT + 16, :].reshape(128, 128)
    picked = dot_nt(stat_block(joint, delta).astype(BF), subset_pick(6, 4))
    payload_ref[256:, :] = widen_stats(picked)


def level_two(block_ref, payload_ref, stat_ref, out_t_ref):
    pick = subset_pick(4, 2)
    query, key, value, grad = later_set(block_ref)
    old_log, old_delta = later_stats(block_ref)
    powers, total, new_log, new_delta = set_stats(query, key, value, grad)
    joint, delta = merge(old_log, old_delta, new_log, new_delta)
    weight = (jnp.exp(new_log - joint) / total)[:, :128]
    out_t_ref[...] = dot_tn(value, powers[:, :128].astype(BF)) * weight
    stat_ref[0:1, :] = joint
    stat_ref[1:2, :] = delta
    stat_ref[2:, :] = jnp.zeros((6, ROWS), F32)
    payload_ref[:128, :] = dot_nn(pick, block_ref[:, :128, :].reshape(ROWS, 128)).astype(BF)
    payload_ref[128:256, :] = dot_nn(pick, block_ref[:, 128:256, :].reshape(ROWS, 128)).astype(BF)
    picked = dot_nt(stat_block(joint, delta).astype(BF), pick)
    payload_ref[256:, :] = widen_stats(picked)


def set_grads(data, log_row, delta_row, own):
    query, key, value, grad = data
    probability = jnp.exp(dot_nt(key, query) - log_row)
    score_grad = (probability * (dot_nt(value, grad) - delta_row)).astype(BF)
    key_grad = dot_nn(score_grad[:own], query)
    value_grad = dot_nn(probability[:own].astype(BF), grad)
    query_grad_t = dot_tn(key, score_grad[:, :own]) * SCALE
    return query_grad_t, jnp.concatenate([key_grad, value_grad], axis=1)


def spread_lanes(value, pick):
    high, low = split2(value)
    return dot_nn(high, pick) + dot_nn(low, pick)


def spread_stats(log_row, delta_row, pick):
    return stat_rows(dot_nn(stat_block(log_row, delta_row).astype(BF), pick))


def level_three(first_ref, second_ref, third_ref, stat1_ref, stat2_ref, out1_ref, out2_ref, payload_ref):
    pick2 = subset_pick(6, 4)
    pick3 = subset_pick(4, 2)
    in_second = jnp.sum(pick2.astype(F32), axis=0, keepdims=True) > 0.5
    in_third = jnp.sum(pick3.astype(F32), axis=0, keepdims=True) > 0.5

    data3 = later_set(third_ref)
    query, key, value, grad = data3
    old_log, old_delta = later_stats(third_ref)
    powers, total, new_log, new_delta = set_stats(query, key, value, grad)
    log3, delta3 = merge(old_log, old_delta, new_log, new_delta)
    weight = (jnp.exp(new_log - log3) / total)[:, :128]
    out3 = dot_tn(value, powers[:, :128].astype(BF)) * weight
    dq3, dkv3 = set_grads(data3, log3, delta3, 128)

    spread_log, spread_delta = spread_stats(log3[:, :128], delta3[:, :128], pick3)
    log2 = jnp.where(in_third, spread_log, stat2_ref[0:1, :])
    delta2 = jnp.where(in_third, spread_delta, stat2_ref[1:2, :])
    data2 = later_set(second_ref)
    dq2, dkv2 = set_grads(data2, log2, delta2, 128)
    own3 = pick3[:32, :128]
    own_lane = lax.broadcasted_iota(jnp.int32, (1, 128), 1) < 32
    merged_t = jnp.concatenate([dq3, out3], axis=0)
    merged_t = jnp.where(own_lane, merged_t, 0.0)
    own_pick = jnp.concatenate([own3, jnp.zeros((96, 128), BF)], axis=0)
    fade2 = jnp.exp(stat2_ref[0:1, :128] - log2[:, :128])
    base_t = jnp.concatenate([dq2, out2_ref[...] * fade2], axis=0)
    merged_t = base_t + spread_lanes(merged_t, own_pick)
    high, low = split2(dkv3[:32])
    dkv2 = dkv2 + dot_tn(own3, high) + dot_tn(own3, low)

    spread_log, spread_delta = spread_stats(log2[:, :128], delta2[:, :128], pick2)
    log1 = jnp.where(in_second, spread_log, stat1_ref[0:1, :])
    delta1 = jnp.where(in_second, spread_delta, stat1_ref[1:2, :])
    data1 = first_set(first_ref)
    dq1, dkv1 = set_grads(data1, log1, delta1, ROWS)
    fade1 = jnp.exp(stat1_ref[0:1, :] - log1)
    base_t = jnp.concatenate([dq1, out1_ref[...] * fade1], axis=0)
    merged_t = base_t + spread_lanes(merged_t, pick2)
    high, low = split2(dkv2)
    dkv1 = dkv1 + dot_tn(pick2, high) + dot_tn(pick2, low)

    payload_ref[:, :KEPT, :] = merged_t.T.astype(BF).reshape(8, KEPT, 128)
    payload_ref[:, KEPT:2 * KEPT, :] = dkv1.astype(BF).reshape(8, KEPT, 128)
    stats = stat_block(log1, delta1)
    for owner in range(8):
        payload_ref[owner, 2 * KEPT:, :] = widen_stats(stats[:, owner * KEPT:(owner + 1) * KEPT])


def returned_stats(block):
    return stat_rows(block[2 * KEPT:2 * KEPT + 8, :KEPT])


def kept_attended(info_ref, back_ref, kept_out_ref, kept_log_ref, att_ref):
    for local in range(LOCAL_HEADS):
        block = back_ref[owner_of(info_ref, local)]
        log_total, _ = returned_stats(block)
        fade = jnp.exp(kept_log_ref[local:local + 1, :] - log_total)
        fade = jnp.broadcast_to(fade, (HEAD_DIM, KEPT)).T
        sparse = block[:KEPT, 64:].astype(F32)
        att_ref[:, span(local)] = (kept_out_ref[:, span(local)] * fade + sparse).astype(BF)


def diagonal(first, second):
    zero = jnp.zeros_like(first)
    return jnp.concatenate(
        [jnp.concatenate([first, zero], axis=1), jnp.concatenate([zero, second], axis=1)], axis=0
    )


def tall_pair(half, pair):
    return jnp.concatenate([tall_pick(head_of(half, 2 * pair)), tall_pick(head_of(half, 2 * pair + 1))], axis=1)


def final_grads(info_ref, q_ref, k_ref, v_ref, sent_ref, back_ref, dq_ref, dk_ref, dv_ref,
                dq_out_ref, dk_out_ref, dv_out_ref, held, sems):
    moves = []
    for pair in range(PAIRS):
        sent = [sent_ref[owner_of(info_ref, 2 * pair + spot)] for spot in range(2)]
        back = [back_ref[owner_of(info_ref, 2 * pair + spot)] for spot in range(2)]
        key = k_ref[:, cols(pair)]
        query = diagonal(*(block[:KEPT, :64] * BF(SCALE) for block in sent))
        grad = diagonal(*(block[KEPT:2 * KEPT, 64:] for block in sent))
        stats = [returned_stats(block) for block in back]
        log_total = jnp.concatenate([stat[0] for stat in stats], axis=1)
        delta = jnp.concatenate([stat[1] for stat in stats], axis=1)
        tall = tall_pair(info_ref[0], pair)
        probability = jnp.exp(dot_nt(key, query) - log_total)
        score_grad = (probability * (dot_nt(v_ref[:, cols(pair)], grad) - delta)).astype(BF)
        more_dk = diagonal(*(block[KEPT:2 * KEPT, :64] for block in back))
        more_dv = diagonal(*(block[KEPT:2 * KEPT, 64:] for block in back))
        dk = dot_nn(jnp.concatenate([score_grad, tall], axis=1), jnp.concatenate([query, more_dk], axis=0))
        dv = dot_nn(
            jnp.concatenate([probability.astype(BF), tall], axis=1), jnp.concatenate([grad, more_dv], axis=0)
        )
        crossed = dot_tn(score_grad, key) * SCALE
        more_dq = diagonal(
            crossed[:64, :64] + back[0][:KEPT, :64].astype(F32), crossed[64:, 64:] + back[1][:KEPT, :64].astype(F32)
        )
        dq = dot_nn(jnp.concatenate([tall, tall], axis=1), jnp.concatenate(split2(more_dq), axis=0))
        for which, (base_ref, more, target) in enumerate(
            ((dq_ref, dq, dq_out_ref), (dk_ref, dk, dk_out_ref), (dv_ref, dv, dv_out_ref))
        ):
            held[pair, which] = (base_ref[:, cols(pair)] + more).astype(BF)
            move = pltpu.make_async_copy(held.at[pair, which], target.at[:, cols(pair)], sems.at[pair, which])
            move.start()
            moves.append(move)
    for move in moves:
        move.wait()


def mix_base(own_att_ref, other_att_ref, own_w_ref, other_w_ref, base_ref):
    base_ref[...] = dot_tn(own_att_ref[...], own_w_ref[...]) + dot_tn(other_att_ref[...], other_w_ref[...])


def spread_kept(half, kept_ref):
    return jnp.concatenate(
        [
            dot_nn(
                tall_pair(half, pair), diagonal(kept_ref[:, span(2 * pair)], kept_ref[:, span(2 * pair + 1)])
            ).astype(BF)
            for pair in range(PAIRS)
        ],
        axis=1,
    )


def mix_own(info_ref, base_ref, kept_ref, w_ref, out_ref):
    out_ref[...] = base_ref[...] + dot_nn(spread_kept(info_ref[0], kept_ref), w_ref[...])


def mix_other(info_ref, base_ref, kept_ref, w_ref, out_ref, held, sems):
    rows = spread_kept(1 - info_ref[0], kept_ref)
    moves = []
    for pair in range(PAIRS):
        held[pair] = (base_ref[:, cols(pair)] + dot_nn(rows, w_ref[:, cols(pair)])).astype(BF)
        move = pltpu.make_async_copy(held.at[pair], out_ref.at[:, cols(pair)], sems.at[pair])
        move.start()
        moves.append(move)
    for move in moves:
        move.wait()


def call(kernel, outs, args, flops=0, info=None, after=(), scratch=(), far_in=False, far_out=False):
    shapes = tuple(jax.ShapeDtypeStruct(*out) for out in outs)
    moved = sum(a.size * a.dtype.itemsize for a in args) + sum(
        int(np.prod(shape)) * jnp.dtype(dtype).itemsize for shape, dtype in outs
    )
    scalars = () if info is None else (info,)
    last = len(scalars) + len(args)

    def run(*refs):
        kernel(*refs[:last], *refs[last + len(after):])

    run.__name__ = kernel.__name__
    near, far = pl.BlockSpec(memory_space=pltpu.VMEM), pl.BlockSpec(memory_space=pltpu.HBM)
    return pl.pallas_call(
        run,
        out_shape=shapes,
        in_specs=[pl.BlockSpec(memory_space=pltpu.SMEM)] * len(scalars)
        + [far if far_in else near] * len(args)
        + [pl.BlockSpec(memory_space=pl.ANY)] * len(after),
        out_specs=(far if far_out else near,) * len(outs),
        scratch_shapes=list(scratch),
        compiler_params=pltpu.CompilerParams(vmem_limit_bytes=VMEM_LIMIT),
        cost_estimate=pl.CostEstimate(flops=flops, bytes_accessed=moved, transcendentals=0),
        name=kernel.__name__,
    )(*scalars, *args, *after)


def partner(array):
    return lax.ppermute(array, "head", [(0, 1), (1, 0)])


def flip(array, mask):
    return lax.ppermute(array, "seq", [(i, i ^ mask) for i in range(lax.axis_size("seq"))])


def gather_pair(array, first, second):
    pair = jnp.stack([array, flip(array, first)])
    return jnp.concatenate([pair, flip(pair, second)])


def body(queries, keys, values, weight_out, cotangent):
    seq_count = lax.axis_size("seq")
    half = lax.axis_index("head")
    octets = [[8 * i + j for j in range(8)] for i in range(seq_count // 8)]
    mirror = 6 * (lax.axis_index("seq") // 8 % 2)
    info = jnp.stack([half, mirror]).astype(jnp.int32)

    block = ((8, 2 * KEPT + 16, 128), BF)
    later_block = ((272, 128), BF)
    stat = ((8, ROWS), F32)
    square = ((ROWS, WIDE), F32)

    other_cot = partner(cotangent)
    q, k, v, out_t, log0, att_t, kept_out, kept_log = call(
        local_forward,
        [((ROWS, WIDE), BF)] * 3
        + [((WIDE, ROWS), F32), stat, ((WIDE, ROWS), BF), ((KEPT, WIDE), F32), ((8, KEPT), F32)],
        (queries, keys, values), flops=400000000, info=info,
        scratch=[pltpu.SemaphoreType.DMA((PAIRS, 3))], far_in=True,
    )
    grad, delta0, sent = call(
        pack_rows, [((ROWS, WIDE), BF), stat, block],
        (q, k, v, cotangent, other_cot, weight_out, out_t, log0), flops=600000000, info=info,
    )
    block1 = lax.all_to_all(sent, "seq", 0, 0, axis_index_groups=octets)
    late_w, late_att, _ = lax.optimization_barrier((weight_out, att_t, sent))
    own_w = lax.dynamic_slice_in_dim(late_w, half * WIDE, WIDE, 1)
    mix_w = partner(lax.dynamic_slice_in_dim(late_w, (1 - half) * WIDE, WIDE, 1))
    other_att_t = partner(late_att)

    sent2, stat1, out1 = call(level_one, [later_block, stat, ((64, ROWS), F32)], (block1,), flops=100000000)
    block2 = gather_pair(sent2, 14, 16)
    sent3, stat2, out2 = call(
        level_two, [later_block, stat, ((64, 128), F32)], (block2,), flops=100000000, after=(other_att_t, mix_w)
    )
    block3 = gather_pair(sent3, 64, 48)
    (base,) = call(mix_base, [square], (late_att, other_att_t, own_w, mix_w), flops=300000000)
    (returned,) = call(
        level_three, [block], (block1, block2, block3, stat1, stat2, out1, out2), flops=300000000, after=(base,)
    )
    back = lax.all_to_all(returned, "seq", 0, 0, axis_index_groups=octets)
    dq, dk, dv = call(
        local_backward, [square] * 3, (q, k, v, grad, log0, delta0), flops=1000000000, info=info,
        after=(returned,),
    )
    (own_kept,) = call(
        kept_attended, [((KEPT, WIDE), BF)], (back, kept_out, kept_log), flops=10000000, info=info, after=(dq,)
    )
    other_kept = partner(own_kept)
    query_grad, key_grad, value_grad = call(
        final_grads, [((ROWS, WIDE), BF)] * 3, (q, k, v, sent, back, dq, dk, dv), flops=200000000, info=info,
        scratch=[pltpu.VMEM((PAIRS, 3, ROWS, 128), BF), pltpu.SemaphoreType.DMA((PAIRS, 3))], far_out=True,
    )
    (nearly,) = call(mix_own, [square], (base, own_kept, own_w), flops=200000000, info=info)
    (mixed,) = call(
        mix_other, [((ROWS, WIDE), BF)], (nearly, other_kept, mix_w), flops=200000000, info=info,
        scratch=[pltpu.VMEM((PAIRS, ROWS, 128), BF), pltpu.SemaphoreType.DMA((PAIRS,))], far_out=True,
    )
    return mixed, query_grad, key_grad, value_grad


def solution(mesh):
    specs = P("seq", "head")
    return jax.shard_map(
        body,
        mesh=mesh,
        in_specs=(specs, specs, specs, P("head", None), specs),
        out_specs=(specs, specs, specs, specs),
        check_vma=False,
    )
```

```python
import functools

import jax
import jax.numpy as jnp
import numpy as np
from jax import lax
from jax.experimental import pallas as pl
from jax.experimental.pallas import tpu as pltpu
from jax.sharding import PartitionSpec as P

HEAD_DIM = 64
LOCAL_HEADS = 6
PAIRS = LOCAL_HEADS // 2
ROWS = 512
KEPT = 64
WIDE = 384
SCALE = HEAD_DIM ** -0.5
BF = jnp.bfloat16
F32 = jnp.float32
MASKED = 1e30
VMEM_LIMIT = 24 * 1024 * 1024


def iota(shape, axis):
    return lax.broadcasted_iota(jnp.int32, shape, axis)


def kept_row(place, head):
    phase = lax.shift_right_logical(head, 3)
    third = 16 * place + phase
    later = place - 4
    second = 4 * (later + lax.shift_right_arithmetic(later * 11, 5) + 1) + phase
    last = place - 16
    group = lax.shift_right_arithmetic(last * 171, 9)
    spot = last - 3 * group
    first = 4 * group + spot + jnp.where(spot >= phase, 1, 0)
    chosen = jnp.where(place < 4, third, jnp.where(place < 16, second, first))
    return 8 * chosen + jnp.bitwise_and(head, 7)


def one_hot(match):
    return jnp.where(match, 1.0, 0.0).astype(BF)


def flat_pick(head):
    return one_hot(iota((KEPT, ROWS), 1) == kept_row(iota((KEPT, 1), 0), head))


def tall_pick(head):
    return one_hot(iota((ROWS, KEPT), 0) == kept_row(iota((1, KEPT), 1), head))


def subset_pick(wide, narrow):
    place = iota((128, 1), 0)
    group = lax.shift_right_logical(place, narrow)
    target = lax.shift_left(group, wide) + jnp.bitwise_and(place, (1 << narrow) - 1)
    return one_hot(iota((128, ROWS), 1) == target)


def dot_nn(left, right):
    return lax.dot_general(left, right, (((1,), (0,)), ((), ())), preferred_element_type=F32)


def dot_nt(left, right):
    return lax.dot_general(left, right, (((1,), (1,)), ((), ())), preferred_element_type=F32)


def dot_tn(left, right):
    return lax.dot_general(left, right, (((0,), (0,)), ((), ())), preferred_element_type=F32)


def split2(value):
    high = value.astype(BF)
    return high, (value - high.astype(F32)).astype(BF)


def split3(value):
    high = value.astype(BF)
    rest = value - high.astype(F32)
    middle = rest.astype(BF)
    return high, middle, (rest - middle.astype(F32)).astype(BF)


def stat_block(log_row, delta_row):
    pieces = split3(log_row) + split3(delta_row)
    rows = [piece.astype(F32) for piece in pieces]
    zero = jnp.zeros_like(log_row)
    return jnp.concatenate(rows + [zero, zero], axis=0)


def stat_rows(block):
    block = block.astype(F32)
    log_row = block[0:1] + block[1:2] + block[2:3]
    delta_row = block[3:4] + block[4:5] + block[5:6]
    return log_row, delta_row


def log_add(first, second):
    peak = jnp.maximum(first, second)
    return peak + jnp.log(jnp.exp(first - peak) + jnp.exp(second - peak))


def span(local):
    return slice(local * HEAD_DIM, (local + 1) * HEAD_DIM)


def cols(pair):
    return slice(pair * 128, (pair + 1) * 128)


OWNERS = (0, 2, 4, 3, 5, 7)
IDLE = (1, 6)


def slot_of(info_ref, place):
    return jnp.bitwise_xor(info_ref[1], place)


def slot_of_head(info_ref, local):
    return slot_of(info_ref, OWNERS[local])


def head_of(half, local):
    return half * LOCAL_HEADS + local


def diagonal(first, second):
    zero = jnp.zeros_like(first)
    return jnp.concatenate(
        [jnp.concatenate([first, zero], axis=1), jnp.concatenate([zero, second], axis=1)], axis=0
    )


def pack_data(info_ref, qkv_ref, packed_ref, hots_ref):
    for local in range(LOCAL_HEADS):
        hot = flat_pick(head_of(info_ref[0], local))
        hots_ref[span(local), :] = hot
        joined = jnp.concatenate([qkv_ref[part, :, span(local)] for part in range(3)], axis=1)
        rows = dot_nn(hot, joined).astype(BF)
        packed_ref[local, :KEPT, :] = jnp.concatenate([rows[:, :64] * BF(SCALE), rows[:, 64:128]], axis=1)
        packed_ref[local, KEPT:, :] = jnp.concatenate([rows[:, 128:], jnp.zeros((KEPT, 64), BF)], axis=1)


def kept_forward(qkv_ref, packed_ref, out_ref, log_ref):
    log_ref[LOCAL_HEADS:, :] = jnp.zeros((8 - LOCAL_HEADS, KEPT), F32)
    for pair in range(PAIRS):
        query = diagonal(packed_ref[2 * pair, :KEPT, :64], packed_ref[2 * pair + 1, :KEPT, :64])
        scores = dot_nt(qkv_ref[1, :, cols(pair)], query)
        peak = jnp.max(scores, axis=0, keepdims=True)
        powers = jnp.exp(scores - peak)
        total = jnp.sum(powers, axis=0, keepdims=True)
        crossed = (dot_tn(qkv_ref[2, :, cols(pair)], powers.astype(BF)) / total).T
        out_ref[:, cols(pair)] = jnp.concatenate([crossed[:64, :64], crossed[64:, 64:]], axis=1)
        log_row = peak + jnp.log(total)
        log_ref[2 * pair:2 * pair + 1, :] = log_row[:, :64]
        log_ref[2 * pair + 1:2 * pair + 2, :] = log_row[:, 64:]


def pack_grads(info_ref, packed_ref, own_cot_ref, other_cot_ref, w_ref, hots_ref, kept_out_ref,
               kept_log_ref, grad_ref, kept_grad_ref, near_ref, far_ref, slots):
    own_w = w_ref[:, pl.ds(pl.multiple_of(info_ref[0] * WIDE, 128), WIDE)]
    other_w = w_ref[:, pl.ds(pl.multiple_of((1 - info_ref[0]) * WIDE, 128), WIDE)]
    grad = (dot_nt(own_cot_ref[...], own_w) + dot_nt(other_cot_ref[...], other_w)).astype(BF)
    grad_ref[...] = grad
    for local in range(LOCAL_HEADS):
        rows = dot_nn(hots_ref[span(local), :], grad[:, span(local)])
        kept_grad = rows.astype(BF)
        kept_grad_ref[:, span(local)] = kept_grad
        delta = jnp.sum((rows * kept_out_ref[:, span(local)]).T, axis=0, keepdims=True)
        slot = slot_of_head(info_ref, local)
        slots[slot, :KEPT, :] = packed_ref[local, :KEPT, :]
        slots[slot, KEPT:2 * KEPT, :] = jnp.concatenate([packed_ref[local, KEPT:, :64], kept_grad], axis=1)
        slots[slot, 2 * KEPT:, :] = widen_stats(stat_block(kept_log_ref[local:local + 1, :], delta))
    for spare in IDLE:
        slots[slot_of(info_ref, spare)] = jnp.zeros((2 * KEPT + 16, 128), BF)
    for chip in range(4):
        near_ref[chip] = slots[2 * chip]
        far_ref[chip] = slots[2 * chip + 1]


def local_forward(info_ref, qkv_ref, out_t_ref, log_ref, att_t_ref):
    log_ref[LOCAL_HEADS:, :] = jnp.zeros((8 - LOCAL_HEADS, ROWS), F32)
    for local in range(LOCAL_HEADS):
        scores = dot_nt(qkv_ref[1, :, span(local)], qkv_ref[0, :, span(local)] * BF(SCALE))
        peak = jnp.max(scores, axis=0, keepdims=True)
        powers = jnp.exp(scores - peak)
        total = jnp.sum(powers, axis=0, keepdims=True)
        out_t = dot_tn(qkv_ref[2, :, span(local)], powers.astype(BF)) / total
        log_row = peak + jnp.log(total)
        out_t_ref[span(local), :] = out_t
        log_ref[local:local + 1, :] = log_row
        head = head_of(info_ref[0], local)
        is_kept = jnp.bitwise_and(iota((1, ROWS), 1), 7) == jnp.bitwise_and(head, 7)
        att_t_ref[span(local), :] = jnp.where(is_kept, 0.0, out_t).astype(BF)


def widen_stats(block):
    if block.shape[1] < 128:
        block = jnp.concatenate([block, jnp.zeros((8, 128 - block.shape[1]), F32)], axis=1)
    return jnp.concatenate([block, jnp.zeros((8, 128), F32)], axis=0).astype(BF)


def local_backward(pair, info_ref, qkv_ref, grad_ref, log_ref, out_t_ref, dq_ref, dk_ref, dv_ref):
    dq_t, dk, dv = [], [], []
    for local in (2 * pair, 2 * pair + 1):
        query = qkv_ref[0, :, span(local)] * BF(SCALE)
        key = qkv_ref[1, :, span(local)]
        grad = grad_ref[:, span(local)]
        head = head_of(info_ref[0], local)
        is_kept = jnp.bitwise_and(iota((1, ROWS), 1), 7) == jnp.bitwise_and(head, 7)
        log_row = jnp.where(is_kept, MASKED, log_ref[local:local + 1, :])
        probability = jnp.exp(dot_nt(key, query) - log_row)
        delta = jnp.sum(grad.astype(F32).T * out_t_ref[span(local), :], axis=0, keepdims=True)
        score_grad = probability * (dot_nt(qkv_ref[2, :, span(local)], grad) - delta)
        score_grad = score_grad.astype(BF)
        dv.append(dot_nn(probability.astype(BF), grad))
        dk.append(dot_nn(score_grad, query))
        dq_t.append(dot_tn(key, score_grad))
    dq_ref[...] = jnp.concatenate(dq_t, axis=0).T * SCALE
    dk_ref[...] = jnp.concatenate(dk, axis=1)
    dv_ref[...] = jnp.concatenate(dv, axis=1)


def set_stats(query, key, value, grad):
    scores = dot_nt(key, query)
    peak = jnp.max(scores, axis=0, keepdims=True)
    powers = jnp.exp(scores - peak)
    total = jnp.sum(powers, axis=0, keepdims=True)
    prob_grad = dot_nt(value, grad)
    delta = jnp.sum(powers * prob_grad, axis=0, keepdims=True) / total
    return scores, prob_grad, powers, total, peak + jnp.log(total), delta


def merge(old_log, old_delta, new_log, new_delta):
    joint = log_add(old_log, new_log)
    return joint, jnp.exp(old_log - joint) * old_delta + jnp.exp(new_log - joint) * new_delta


def first_set(block_ref):
    joined = block_ref[:, :KEPT, :].reshape(ROWS, 128)
    other = block_ref[:, KEPT:2 * KEPT, :].reshape(ROWS, 128)
    return joined[:, :64], joined[:, 64:], other[:, :64], other[:, 64:]


def later_set(block_ref):
    joined = block_ref[:, :128, :].reshape(ROWS, 128)
    other = block_ref[:, 128:256, :].reshape(ROWS, 128)
    return joined[:, :64], joined[:, 64:], other[:, :64], other[:, 64:]


def later_stats(block_ref):
    return stat_rows(jnp.concatenate([block_ref[i, 256:264, :].astype(F32) for i in range(4)], axis=1))


def level_one(block_ref, payload_ref, stat_ref, out_t_ref):
    query, key, value, grad = first_set(block_ref)
    stats = jnp.concatenate([block_ref[i, 128:136, :KEPT].astype(F32) for i in range(8)], axis=1)
    old_log, old_delta = stat_rows(stats)
    _, _, powers, total, new_log, new_delta = set_stats(query, key, value, grad)
    joint, delta = merge(old_log, old_delta, new_log, new_delta)
    out_t_ref[...] = dot_tn(value, powers.astype(BF)) * (jnp.exp(new_log - joint) / total)
    stat_ref[0:1, :] = joint
    stat_ref[1:2, :] = delta
    stat_ref[2:, :] = jnp.zeros((6, ROWS), F32)
    payload_ref[:128, :] = block_ref[:, :16, :].reshape(128, 128)
    payload_ref[128:256, :] = block_ref[:, KEPT:KEPT + 16, :].reshape(128, 128)
    picked = dot_nt(stat_block(joint, delta).astype(BF), subset_pick(6, 4))
    payload_ref[256:, :] = widen_stats(picked)


def level_two(block_ref, payload_ref, stat_ref, out_t_ref):
    pick = subset_pick(4, 2)
    query, key, value, grad = later_set(block_ref)
    old_log, old_delta = later_stats(block_ref)
    _, _, powers, total, new_log, new_delta = set_stats(query, key, value, grad)
    joint, delta = merge(old_log, old_delta, new_log, new_delta)
    weight = (jnp.exp(new_log - joint) / total)[:, :128]
    out_t_ref[...] = dot_tn(value, powers[:, :128].astype(BF)) * weight
    stat_ref[0:1, :] = joint
    stat_ref[1:2, :] = delta
    stat_ref[2:, :] = jnp.zeros((6, ROWS), F32)
    payload_ref[:128, :] = dot_nn(pick, block_ref[:, :128, :].reshape(ROWS, 128)).astype(BF)
    payload_ref[128:256, :] = dot_nn(pick, block_ref[:, 128:256, :].reshape(ROWS, 128)).astype(BF)
    picked = dot_nt(stat_block(joint, delta).astype(BF), pick)
    payload_ref[256:, :] = widen_stats(picked)


def weigh(query, key, value, grad, log_row, delta_row):
    probability = jnp.exp(dot_nt(key, query) - log_row)
    score_grad = probability * (dot_nt(value, grad) - delta_row)
    return probability.astype(BF), score_grad.astype(BF)


def key_side(probability, score_grad, query, grad):
    return jnp.concatenate([dot_nn(score_grad, query), dot_nn(probability, grad)], axis=1)


def runs(lanes, wide, narrow):
    return jnp.bitwise_and(iota((1, lanes), 1), wide - 1) < narrow


def level_one_back(block_ref, stat_ref, dq_ref, dkv_ref):
    query, key, value, grad = first_set(block_ref)
    log_row = jnp.where(runs(ROWS, 64, 16), MASKED, stat_ref[0:1, :])
    probability, score_grad = weigh(query, key, value, grad, log_row, stat_ref[1:2, :])
    dq_ref[...] = dot_tn(key, score_grad) * SCALE
    dkv_ref[...] = key_side(probability, score_grad, query, grad)


def level_two_back(first_ref, second_ref, stat_ref, dkv1_ref, dkv1_out_ref, dkv2_ref, dq_ref):
    _, key1, value1, _ = first_set(first_ref)
    query, key, value, grad = later_set(second_ref)
    log_row = jnp.where(runs(ROWS, 16, 4), MASKED, stat_ref[0:1, :])
    delta_row = stat_ref[1:2, :]
    own_query, own_grad = query[:128], grad[:128]
    probability, score_grad = weigh(own_query, key1, value1, own_grad, log_row[:, :128], delta_row[:, :128])
    dkv1_out_ref[...] = dkv1_ref[...] + key_side(probability, score_grad, own_query, own_grad)
    dq = dot_tn(key1, score_grad)
    probability, score_grad = weigh(query, key, value, grad, log_row, delta_row)
    dkv2_ref[...] = key_side(probability[:128], score_grad[:128], query, grad)
    dq_ref[...] = (dq + dot_tn(key, score_grad[:, :128])) * SCALE


def spread_lanes(value, pick):
    high, low = split2(value)
    return dot_nn(high, pick) + dot_nn(low, pick)


def spread_stats(log_row, delta_row, pick):
    return stat_rows(dot_nn(stat_block(log_row, delta_row).astype(BF), pick))


def level_three(first_ref, second_ref, third_ref, stat1_ref, stat2_ref, out1_ref, out2_ref, dq1_ref, dkv1_ref,
                dq2_ref, dkv2_ref, near_ref, far_ref):
    pick2 = subset_pick(6, 4)
    own_lane = iota((1, 128), 1) < 32

    query, key, value, grad = later_set(third_ref)
    old_log, old_delta = later_stats(third_ref)
    scores, prob_grad, powers, total, new_log, new_delta = set_stats(query, key, value, grad)
    log3, delta3 = merge(old_log, old_delta, new_log, new_delta)
    weight = (jnp.exp(new_log - log3) / total)[:, :128]
    out3 = dot_tn(value, powers[:, :128].astype(BF)) * weight
    own_query, own_grad = query[:128], grad[:128]
    own_log, own_delta = log3[:, :128], delta3[:, :128]

    _, key1, value1, _ = first_set(first_ref)
    octet_log = jnp.where(own_lane, own_log, MASKED)
    probability, score_grad = weigh(own_query, key1, value1, own_grad, octet_log, own_delta)
    dkv1 = dkv1_ref[...] + key_side(probability, score_grad, own_query, own_grad)
    dq = dot_tn(key1, score_grad)
    _, key2, value2, _ = later_set(second_ref)
    probability, score_grad = weigh(own_query, key2, value2, own_grad, own_log, own_delta)
    dkv2 = dkv2_ref[...] + key_side(probability[:128], score_grad[:128], own_query, own_grad)
    dq = dq + dot_tn(key2, score_grad)
    probability = jnp.exp(scores[:, :128] - own_log)
    dq = dq + dot_tn(key, (probability * (prob_grad[:, :128] - own_delta)).astype(BF))
    probability = jnp.exp(scores[:32] - log3)
    score_grad = (probability * (prob_grad[:32] - delta3)).astype(BF)
    dkv3 = key_side(probability.astype(BF), score_grad, query, grad)

    place = iota((128, 1), 0)
    target = lax.shift_left(lax.shift_right_logical(place, 2), 4) + jnp.bitwise_and(place, 3)
    own_pick = one_hot((iota((128, 128), 1) == target) & (place < 32))
    spread_log, spread_delta = spread_stats(own_log, own_delta, own_pick)
    in_third = runs(128, 16, 4)
    log2 = jnp.where(in_third, spread_log, stat2_ref[0:1, :128])
    delta2 = jnp.where(in_third, spread_delta, stat2_ref[1:2, :128])
    merged_t = jnp.where(own_lane, jnp.concatenate([dq * SCALE, out3], axis=0), 0.0)
    fade2 = jnp.exp(stat2_ref[0:1, :128] - log2)
    base_t = jnp.concatenate([dq2_ref[...], out2_ref[...] * fade2], axis=0)
    merged_t = base_t + spread_lanes(merged_t, own_pick)
    high, low = split2(dkv3)
    dkv2 = dkv2 + dot_tn(own_pick[:32], high) + dot_tn(own_pick[:32], low)

    spread_log, spread_delta = spread_stats(log2, delta2, pick2)
    in_second = runs(ROWS, 64, 16)
    log1 = jnp.where(in_second, spread_log, stat1_ref[0:1, :])
    delta1 = jnp.where(in_second, spread_delta, stat1_ref[1:2, :])
    fade1 = jnp.exp(stat1_ref[0:1, :] - log1)
    base_t = jnp.concatenate([dq1_ref[...], out1_ref[...] * fade1], axis=0)
    merged_t = base_t + spread_lanes(merged_t, pick2)
    high, low = split2(dkv2)
    dkv1 = dkv1 + dot_tn(pick2, high) + dot_tn(pick2, low)

    rows = merged_t.T.astype(BF)
    dkv1 = dkv1.astype(BF)
    stats = stat_block(log1, delta1)
    for slot in range(8):
        part = slice(slot * KEPT, (slot + 1) * KEPT)
        target_ref = far_ref if slot % 2 else near_ref
        target_ref[slot // 2, :KEPT, :] = rows[part]
        target_ref[slot // 2, KEPT:2 * KEPT, :] = dkv1[part]
        target_ref[slot // 2, 2 * KEPT:, :] = widen_stats(stats[:, part])


def returned_stats(block):
    return stat_rows(block[2 * KEPT:2 * KEPT + 8, :KEPT])


def kept_attended(info_ref, back_ref, kept_out_ref, kept_log_ref, att_ref):
    for local in range(LOCAL_HEADS):
        block = back_ref[slot_of_head(info_ref, local)]
        log_total, _ = returned_stats(block)
        fade = jnp.exp(kept_log_ref[local:local + 1, :] - log_total)
        fade = jnp.broadcast_to(fade, (HEAD_DIM, KEPT)).T
        sparse = block[:KEPT, 64:].astype(F32)
        att_ref[:, span(local)] = (kept_out_ref[:, span(local)] * fade + sparse).astype(BF)


def tall_pair(half, pair):
    return jnp.concatenate([tall_pick(head_of(half, 2 * pair)), tall_pick(head_of(half, 2 * pair + 1))], axis=1)


def final_grads(info_ref, qkv_ref, packed_ref, kept_grad_ref, back_ref, tall_ref, *rest):
    early, (dq_out_ref, dk_out_ref, dv_out_ref, held, sems) = rest[:9], rest[9:]
    moves = []
    for pair in range(PAIRS):
        back = [back_ref[slot_of_head(info_ref, 2 * pair + spot)] for spot in range(2)]
        key = qkv_ref[1, :, cols(pair)]
        query = diagonal(packed_ref[2 * pair, :KEPT, :64], packed_ref[2 * pair + 1, :KEPT, :64])
        grad = diagonal(kept_grad_ref[:, span(2 * pair)], kept_grad_ref[:, span(2 * pair + 1)])
        stats = [returned_stats(block) for block in back]
        log_total = jnp.concatenate([stat[0] for stat in stats], axis=1)
        delta = jnp.concatenate([stat[1] for stat in stats], axis=1)
        tall = tall_ref[:, cols(pair)]
        probability = jnp.exp(dot_nt(key, query) - log_total)
        score_grad = (probability * (dot_nt(qkv_ref[2, :, cols(pair)], grad) - delta)).astype(BF)
        more_dk = diagonal(*(block[KEPT:2 * KEPT, :64] for block in back))
        more_dv = diagonal(*(block[KEPT:2 * KEPT, 64:] for block in back))
        dk = dot_nn(jnp.concatenate([score_grad, tall], axis=1), jnp.concatenate([query, more_dk], axis=0))
        dv = dot_nn(
            jnp.concatenate([probability.astype(BF), tall], axis=1), jnp.concatenate([grad, more_dv], axis=0)
        )
        crossed = dot_tn(score_grad, key) * SCALE
        more_dq = diagonal(
            crossed[:64, :64] + back[0][:KEPT, :64].astype(F32), crossed[64:, 64:] + back[1][:KEPT, :64].astype(F32)
        )
        dq = dot_nn(jnp.concatenate([tall, tall], axis=1), jnp.concatenate(split2(more_dq), axis=0))
        for which, (more, target) in enumerate(((dq, dq_out_ref), (dk, dk_out_ref), (dv, dv_out_ref))):
            held[pair, which] = (early[3 * pair + which][...] + more).astype(BF)
            move = pltpu.make_async_copy(held.at[pair, which], target.at[:, cols(pair)], sems.at[pair, which])
            move.start()
            moves.append(move)
    for move in moves:
        move.wait()


def mix_base(info_ref, own_att_ref, other_att_ref, own_w_ref, other_w_ref, base_ref, own_tall_ref, other_tall_ref):
    base_ref[...] = dot_tn(own_att_ref[...], own_w_ref[...]) + dot_tn(other_att_ref[...], other_w_ref[...])
    for pair in range(PAIRS):
        own_tall_ref[:, cols(pair)] = tall_pair(info_ref[0], pair)
        other_tall_ref[:, cols(pair)] = tall_pair(1 - info_ref[0], pair)


def spread_kept(tall_ref, kept_ref):
    return jnp.concatenate(
        [
            dot_nn(
                tall_ref[:, cols(pair)], diagonal(kept_ref[:, span(2 * pair)], kept_ref[:, span(2 * pair + 1)])
            ).astype(BF)
            for pair in range(PAIRS)
        ],
        axis=1,
    )


def mix_own(base_ref, kept_ref, tall_ref, w_ref, out_ref):
    out_ref[...] = base_ref[...] + dot_nn(spread_kept(tall_ref, kept_ref), w_ref[...])


def mix_other(base_ref, kept_ref, tall_ref, w_ref, out_ref, held, sems):
    rows = spread_kept(tall_ref, kept_ref)
    moves = []
    for pair in range(PAIRS):
        held[pair] = (base_ref[:, cols(pair)] + dot_nn(rows, w_ref[:, cols(pair)])).astype(BF)
        move = pltpu.make_async_copy(held.at[pair], out_ref.at[:, cols(pair)], sems.at[pair])
        move.start()
        moves.append(move)
    for move in moves:
        move.wait()


def call(kernel, outs, args, flops=0, info=None, after=(), scratch=(), far_out=False):
    shapes = tuple(jax.ShapeDtypeStruct(*out) for out in outs)
    moved = sum(a.size * a.dtype.itemsize for a in args) + sum(
        int(np.prod(shape)) * jnp.dtype(dtype).itemsize for shape, dtype in outs
    )
    scalars = () if info is None else (info,)
    last = len(scalars) + len(args)

    def run(*refs):
        kernel(*refs[:last], *refs[last + len(after):])

    name = getattr(kernel, "func", kernel).__name__
    run.__name__ = name
    near, far = pl.BlockSpec(memory_space=pltpu.VMEM), pl.BlockSpec(memory_space=pltpu.HBM)
    return pl.pallas_call(
        run,
        out_shape=shapes,
        in_specs=[pl.BlockSpec(memory_space=pltpu.SMEM)] * len(scalars)
        + [near] * len(args)
        + [pl.BlockSpec(memory_space=pl.ANY)] * len(after),
        out_specs=(far if far_out else near,) * len(outs),
        scratch_shapes=list(scratch),
        compiler_params=pltpu.CompilerParams(vmem_limit_bytes=VMEM_LIMIT),
        cost_estimate=pl.CostEstimate(flops=flops, bytes_accessed=moved, transcendentals=0),
        name=name,
    )(*scalars, *args, *after)


def partner(array):
    return lax.ppermute(array, "head", [(0, 1), (1, 0)])


def flip(array, mask):
    return lax.ppermute(array, "seq", [(i, i ^ mask) for i in range(lax.axis_size("seq"))])


def gather_pair(array, first, second):
    return jnp.stack([array, flip(array, first), flip(array, second), flip(array, first ^ second)])


def octet_exchange(near, far):
    crossed = flip(far, 1)
    blocks = [jnp.stack([near[chip], crossed[chip]]) for chip in range(4)]
    arrived = [flip(blocks[chip], 2 * chip) for chip in (1, 2, 3)]
    return jnp.concatenate([blocks[0]] + arrived), blocks[3], arrived[0]


def body(queries, keys, values, weight_out, cotangent):
    half = lax.axis_index("head")
    place = lax.axis_index("seq")
    info = jnp.stack([half, jnp.bitwise_xor(place % 8, 6 * (place // 8 % 2))]).astype(jnp.int32)

    block = ((4, 2 * KEPT + 16, 128), BF)
    later_block = ((272, 128), BF)
    stat = ((8, ROWS), F32)
    square = ((ROWS, WIDE), F32)

    other_cot = partner(cotangent)
    qkv = jnp.stack([queries, keys, values])
    packed, hots = call(
        pack_data, [((LOCAL_HEADS, 2 * KEPT, 128), BF), ((WIDE, ROWS), BF)], (qkv,), flops=200000000, info=info
    )
    kept_out, kept_log = call(
        kept_forward, [((KEPT, WIDE), F32), ((8, KEPT), F32)], (qkv, packed), flops=100000000
    )
    out_t, log0, att_t = call(
        local_forward, [((WIDE, ROWS), F32), stat, ((WIDE, ROWS), BF)], (qkv,), flops=400000000, info=info,
    )
    grad, kept_grad, near, far = call(
        pack_grads, [((ROWS, WIDE), BF), ((KEPT, WIDE), BF), block, block],
        (packed, cotangent, other_cot, weight_out, hots, kept_out, kept_log), flops=400000000, info=info, after=(att_t,),
        scratch=[pltpu.VMEM((8, 2 * KEPT + 16, 128), BF)],
    )
    block1, _, arrived = octet_exchange(near, far)
    late_w, _ = lax.optimization_barrier((weight_out, near))
    late_att, _ = lax.optimization_barrier((att_t, arrived))
    own_w = lax.dynamic_slice_in_dim(late_w, half * WIDE, WIDE, 1)
    mix_w = partner(lax.dynamic_slice_in_dim(late_w, (1 - half) * WIDE, WIDE, 1))
    other_att_t = partner(late_att)

    half_rows = ((128, 128), F32)

    def backward(pair, after):
        return call(
            functools.partial(local_backward, pair), [((ROWS, 128), F32)] * 3, (qkv, grad, log0, out_t),
            flops=300000000, info=info, after=(after,),
        )

    sent2, stat1, out1 = call(
        level_one, [later_block, stat, ((64, ROWS), F32)], (block1,), flops=100000000
    )
    block2 = gather_pair(sent2, 14, 16)
    dq1, dkv1 = call(level_one_back, [((64, ROWS), F32), ((ROWS, 128), F32)], (block1, stat1), flops=100000000)
    early = list(backward(0, sent2))
    sent3, stat2, out2 = call(
        level_two, [later_block, stat, ((64, 128), F32)], (block2,), flops=100000000,
        after=(other_att_t, mix_w, dq1, early[-1]),
    )
    block3 = gather_pair(sent3, 64, 48)
    early.extend(backward(1, sent3))
    dkv1, dkv2, dq2 = call(
        level_two_back, [((ROWS, 128), F32), half_rows, ((64, 128), F32)], (block1, block2, stat2, dkv1),
        flops=100000000,
    )
    base, own_tall, other_tall = call(
        mix_base, [square, ((ROWS, WIDE), BF), ((ROWS, WIDE), BF)],
        (late_att, other_att_t, own_w, mix_w), flops=300000000, info=info,
    )
    near, far = call(
        level_three, [block, block],
        (block1, block2, block3, stat1, stat2, out1, out2, dq1, dkv1, dq2, dkv2), flops=300000000, after=(base, early[-1]),
    )
    back, crossed, _ = octet_exchange(near, far)
    early.extend(backward(2, crossed))
    (own_kept,) = call(
        kept_attended, [((KEPT, WIDE), BF)], (back, kept_out, kept_log), flops=10000000, info=info, after=(early[-1],)
    )
    other_kept = partner(own_kept)
    query_grad, key_grad, value_grad = call(
        final_grads, [((ROWS, WIDE), BF)] * 3, (qkv, packed, kept_grad, back, own_tall, *early),
        flops=200000000, info=info,
        scratch=[pltpu.VMEM((PAIRS, 3, ROWS, 128), BF), pltpu.SemaphoreType.DMA((PAIRS, 3))], far_out=True,
    )
    (nearly,) = call(mix_own, [square], (base, own_kept, own_tall, own_w), flops=200000000)
    (mixed,) = call(
        mix_other, [((ROWS, WIDE), BF)], (nearly, other_kept, other_tall, mix_w), flops=200000000,
        scratch=[pltpu.VMEM((PAIRS, ROWS, 128), BF), pltpu.SemaphoreType.DMA((PAIRS,))], far_out=True,
    )
    return mixed, query_grad, key_grad, value_grad


def solution(mesh):
    specs = P("seq", "head")
    return jax.shard_map(
        body,
        mesh=mesh,
        in_specs=(specs, specs, specs, P("head", None), specs),
        out_specs=(specs, specs, specs, specs),
        check_vma=False,
    )
```

```python
import functools

import jax
import jax.numpy as jnp
import numpy as np
from jax import lax
from jax.experimental import pallas as pl
from jax.experimental.pallas import tpu as pltpu
from jax.sharding import PartitionSpec as P

HEAD_DIM = 64
LOCAL_HEADS = 6
PAIRS = LOCAL_HEADS // 2
ROWS = 512
KEPT = 64
WIDE = 384
SCALE = HEAD_DIM ** -0.5
BF = jnp.bfloat16
F32 = jnp.float32
MASKED = 1e30
VMEM_LIMIT = 24 * 1024 * 1024


def iota(shape, axis):
    return lax.broadcasted_iota(jnp.int32, shape, axis)


def kept_row(place, head):
    phase = lax.shift_right_logical(head, 3)
    third = 16 * place + phase
    later = place - 4
    second = 4 * (later + lax.shift_right_arithmetic(later * 11, 5) + 1) + phase
    last = place - 16
    group = lax.shift_right_arithmetic(last * 171, 9)
    spot = last - 3 * group
    first = 4 * group + spot + jnp.where(spot >= phase, 1, 0)
    chosen = jnp.where(place < 4, third, jnp.where(place < 16, second, first))
    return 8 * chosen + jnp.bitwise_and(head, 7)


def one_hot(match):
    return jnp.where(match, 1.0, 0.0).astype(BF)


def flat_pick(head):
    return one_hot(iota((KEPT, ROWS), 1) == kept_row(iota((KEPT, 1), 0), head))


def tall_pick(head):
    return one_hot(iota((ROWS, KEPT), 0) == kept_row(iota((1, KEPT), 1), head))


def subset_pick(wide, narrow):
    place = iota((128, 1), 0)
    group = lax.shift_right_logical(place, narrow)
    target = lax.shift_left(group, wide) + jnp.bitwise_and(place, (1 << narrow) - 1)
    return one_hot(iota((128, ROWS), 1) == target)


def dot_nn(left, right):
    return lax.dot_general(left, right, (((1,), (0,)), ((), ())), preferred_element_type=F32)


def dot_nt(left, right):
    return lax.dot_general(left, right, (((1,), (1,)), ((), ())), preferred_element_type=F32)


def dot_tn(left, right):
    return lax.dot_general(left, right, (((0,), (0,)), ((), ())), preferred_element_type=F32)


def split2(value):
    high = value.astype(BF)
    return high, (value - high.astype(F32)).astype(BF)


def split3(value):
    high = value.astype(BF)
    rest = value - high.astype(F32)
    middle = rest.astype(BF)
    return high, middle, (rest - middle.astype(F32)).astype(BF)


def stat_block(log_row, delta_row):
    pieces = split3(log_row) + split3(delta_row)
    rows = [piece.astype(F32) for piece in pieces]
    zero = jnp.zeros_like(log_row)
    return jnp.concatenate(rows + [zero, zero], axis=0)


def stat_rows(block):
    block = block.astype(F32)
    log_row = block[0:1] + block[1:2] + block[2:3]
    delta_row = block[3:4] + block[4:5] + block[5:6]
    return log_row, delta_row


def log_add(first, second):
    peak = jnp.maximum(first, second)
    return peak + jnp.log(jnp.exp(first - peak) + jnp.exp(second - peak))


def span(local):
    return slice(local * HEAD_DIM, (local + 1) * HEAD_DIM)


def cols(pair):
    return slice(pair * 128, (pair + 1) * 128)


OWNERS = (0, 2, 4, 3, 5, 7)
IDLE = (1, 6)


def slot_of(info_ref, place):
    return jnp.bitwise_xor(info_ref[1], place)


def slot_of_head(info_ref, local):
    return slot_of(info_ref, OWNERS[local])


def head_of(half, local):
    return half * LOCAL_HEADS + local


def diagonal(first, second):
    zero = jnp.zeros_like(first)
    return jnp.concatenate(
        [jnp.concatenate([first, zero], axis=1), jnp.concatenate([zero, second], axis=1)], axis=0
    )


def pack_data(info_ref, qkv_ref, packed_ref, hots_ref):
    for local in range(LOCAL_HEADS):
        hot = flat_pick(head_of(info_ref[0], local))
        hots_ref[span(local), :] = hot
        joined = jnp.concatenate([qkv_ref[part, :, span(local)] for part in range(3)], axis=1)
        rows = dot_nn(hot, joined).astype(BF)
        packed_ref[local, :KEPT, :] = jnp.concatenate([rows[:, :64] * BF(SCALE), rows[:, 64:128]], axis=1)
        packed_ref[local, KEPT:, :] = jnp.concatenate([rows[:, 128:], jnp.zeros((KEPT, 64), BF)], axis=1)


def kept_forward(qkv_ref, packed_ref, out_ref, log_ref):
    log_ref[LOCAL_HEADS:, :] = jnp.zeros((8 - LOCAL_HEADS, KEPT), F32)
    for pair in range(PAIRS):
        query = diagonal(packed_ref[2 * pair, :KEPT, :64], packed_ref[2 * pair + 1, :KEPT, :64])
        scores = dot_nt(qkv_ref[1, :, cols(pair)], query)
        peak = jnp.max(scores, axis=0, keepdims=True)
        powers = jnp.exp(scores - peak)
        total = jnp.sum(powers, axis=0, keepdims=True)
        crossed = (dot_tn(qkv_ref[2, :, cols(pair)], powers.astype(BF)) / total).T
        out_ref[:, cols(pair)] = jnp.concatenate([crossed[:64, :64], crossed[64:, 64:]], axis=1)
        log_row = peak + jnp.log(total)
        log_ref[2 * pair:2 * pair + 1, :] = log_row[:, :64]
        log_ref[2 * pair + 1:2 * pair + 2, :] = log_row[:, 64:]


def pack_grads(info_ref, packed_ref, own_cot_ref, other_cot_ref, w_ref, hots_ref, kept_out_ref,
               kept_log_ref, grad_ref, kept_grad_ref, near_ref, far_ref, slots):
    own_w = w_ref[:, pl.ds(pl.multiple_of(info_ref[0] * WIDE, 128), WIDE)]
    other_w = w_ref[:, pl.ds(pl.multiple_of((1 - info_ref[0]) * WIDE, 128), WIDE)]
    grad = (dot_nt(own_cot_ref[...], own_w) + dot_nt(other_cot_ref[...], other_w)).astype(BF)
    grad_ref[...] = grad
    for local in range(LOCAL_HEADS):
        rows = dot_nn(hots_ref[span(local), :], grad[:, span(local)])
        kept_grad = rows.astype(BF)
        kept_grad_ref[:, span(local)] = kept_grad
        delta = jnp.sum((rows * kept_out_ref[:, span(local)]).T, axis=0, keepdims=True)
        slot = slot_of_head(info_ref, local)
        slots[slot, :KEPT, :] = packed_ref[local, :KEPT, :]
        slots[slot, KEPT:2 * KEPT, :] = jnp.concatenate([packed_ref[local, KEPT:, :64], kept_grad], axis=1)
        slots[slot, 2 * KEPT:, :] = widen_stats(stat_block(kept_log_ref[local:local + 1, :], delta))
    for spare in IDLE:
        slots[slot_of(info_ref, spare)] = jnp.zeros((2 * KEPT + 16, 128), BF)
    for chip in range(4):
        near_ref[chip] = slots[2 * chip]
        far_ref[chip] = slots[2 * chip + 1]


def local_forward(info_ref, qkv_ref, out_t_ref, log_ref, att_t_ref):
    log_ref[LOCAL_HEADS:, :] = jnp.zeros((8 - LOCAL_HEADS, ROWS), F32)
    for local in range(LOCAL_HEADS):
        scores = dot_nt(qkv_ref[1, :, span(local)], qkv_ref[0, :, span(local)] * BF(SCALE))
        peak = jnp.max(scores, axis=0, keepdims=True)
        powers = jnp.exp(scores - peak)
        total = jnp.sum(powers, axis=0, keepdims=True)
        out_t = dot_tn(qkv_ref[2, :, span(local)], powers.astype(BF)) / total
        log_row = peak + jnp.log(total)
        out_t_ref[span(local), :] = out_t
        log_ref[local:local + 1, :] = log_row
        head = head_of(info_ref[0], local)
        is_kept = jnp.bitwise_and(iota((1, ROWS), 1), 7) == jnp.bitwise_and(head, 7)
        att_t_ref[span(local), :] = jnp.where(is_kept, 0.0, out_t).astype(BF)


def widen_stats(block):
    if block.shape[1] < 128:
        block = jnp.concatenate([block, jnp.zeros((8, 128 - block.shape[1]), F32)], axis=1)
    return jnp.concatenate([block, jnp.zeros((8, 128), F32)], axis=0).astype(BF)


def local_backward(pair, info_ref, qkv_ref, grad_ref, log_ref, out_t_ref, dq_ref, dk_ref, dv_ref):
    dq_t, dk, dv = [], [], []
    for local in (2 * pair, 2 * pair + 1):
        query = qkv_ref[0, :, span(local)] * BF(SCALE)
        key = qkv_ref[1, :, span(local)]
        grad = grad_ref[:, span(local)]
        head = head_of(info_ref[0], local)
        is_kept = jnp.bitwise_and(iota((1, ROWS), 1), 7) == jnp.bitwise_and(head, 7)
        log_row = jnp.where(is_kept, MASKED, log_ref[local:local + 1, :])
        probability = jnp.exp(dot_nt(key, query) - log_row)
        delta = jnp.sum(grad.astype(F32).T * out_t_ref[span(local), :], axis=0, keepdims=True)
        score_grad = probability * (dot_nt(qkv_ref[2, :, span(local)], grad) - delta)
        score_grad = score_grad.astype(BF)
        dv.append(dot_nn(probability.astype(BF), grad))
        dk.append(dot_nn(score_grad, query))
        dq_t.append(dot_tn(key, score_grad))
    dq_ref[...] = jnp.concatenate(dq_t, axis=0).T * SCALE
    dk_ref[...] = jnp.concatenate(dk, axis=1)
    dv_ref[...] = jnp.concatenate(dv, axis=1)


def set_stats(query, key, value, grad):
    scores = dot_nt(key, query)
    peak = jnp.max(scores, axis=0, keepdims=True)
    powers = jnp.exp(scores - peak)
    total = jnp.sum(powers, axis=0, keepdims=True)
    prob_grad = dot_nt(value, grad)
    delta = jnp.sum(powers * prob_grad, axis=0, keepdims=True) / total
    return scores, prob_grad, powers, total, peak + jnp.log(total), delta


def merge(old_log, old_delta, new_log, new_delta):
    joint = log_add(old_log, new_log)
    return joint, jnp.exp(old_log - joint) * old_delta + jnp.exp(new_log - joint) * new_delta


def first_set(block_ref):
    joined = block_ref[:, :KEPT, :].reshape(ROWS, 128)
    other = block_ref[:, KEPT:2 * KEPT, :].reshape(ROWS, 128)
    return joined[:, :64], joined[:, 64:], other[:, :64], other[:, 64:]


def later_set(block_ref):
    joined = block_ref[:, :128, :].reshape(ROWS, 128)
    other = block_ref[:, 128:256, :].reshape(ROWS, 128)
    return joined[:, :64], joined[:, 64:], other[:, :64], other[:, 64:]


def later_stats(block_ref):
    return stat_rows(jnp.concatenate([block_ref[i, 256:264, :].astype(F32) for i in range(4)], axis=1))


def level_one(block_ref, payload_ref, stat_ref, out_t_ref):
    query, key, value, grad = first_set(block_ref)
    stats = jnp.concatenate([block_ref[i, 128:136, :KEPT].astype(F32) for i in range(8)], axis=1)
    old_log, old_delta = stat_rows(stats)
    _, _, powers, total, new_log, new_delta = set_stats(query, key, value, grad)
    joint, delta = merge(old_log, old_delta, new_log, new_delta)
    out_t_ref[...] = dot_tn(value, powers.astype(BF)) * (jnp.exp(new_log - joint) / total)
    stat_ref[0:1, :] = joint
    stat_ref[1:2, :] = delta
    stat_ref[2:, :] = jnp.zeros((6, ROWS), F32)
    payload_ref[:128, :] = block_ref[:, :16, :].reshape(128, 128)
    payload_ref[128:256, :] = block_ref[:, KEPT:KEPT + 16, :].reshape(128, 128)
    picked = dot_nt(stat_block(joint, delta).astype(BF), subset_pick(6, 4))
    payload_ref[256:, :] = widen_stats(picked)


def level_two(block_ref, payload_ref, stat_ref, out_t_ref):
    pick = subset_pick(4, 2)
    query, key, value, grad = later_set(block_ref)
    old_log, old_delta = later_stats(block_ref)
    _, _, powers, total, new_log, new_delta = set_stats(query, key, value, grad)
    joint, delta = merge(old_log, old_delta, new_log, new_delta)
    weight = (jnp.exp(new_log - joint) / total)[:, :128]
    out_t_ref[...] = dot_tn(value, powers[:, :128].astype(BF)) * weight
    stat_ref[0:1, :] = joint
    stat_ref[1:2, :] = delta
    stat_ref[2:, :] = jnp.zeros((6, ROWS), F32)
    payload_ref[:128, :] = dot_nn(pick, block_ref[:, :128, :].reshape(ROWS, 128)).astype(BF)
    payload_ref[128:256, :] = dot_nn(pick, block_ref[:, 128:256, :].reshape(ROWS, 128)).astype(BF)
    picked = dot_nt(stat_block(joint, delta).astype(BF), pick)
    payload_ref[256:, :] = widen_stats(picked)


def weigh(query, key, value, grad, log_row, delta_row):
    probability = jnp.exp(dot_nt(key, query) - log_row)
    score_grad = probability * (dot_nt(value, grad) - delta_row)
    return probability.astype(BF), score_grad.astype(BF)


def key_side(probability, score_grad, query, grad):
    return jnp.concatenate([dot_nn(score_grad, query), dot_nn(probability, grad)], axis=1)


def runs(lanes, wide, narrow):
    return jnp.bitwise_and(iota((1, lanes), 1), wide - 1) < narrow


def level_one_back(block_ref, stat_ref, dq_ref, dkv_ref):
    query, key, value, grad = first_set(block_ref)
    log_row = jnp.where(runs(ROWS, 64, 16), MASKED, stat_ref[0:1, :])
    probability, score_grad = weigh(query, key, value, grad, log_row, stat_ref[1:2, :])
    dq_ref[...] = dot_tn(key, score_grad) * SCALE
    dkv_ref[...] = key_side(probability, score_grad, query, grad)


def level_two_back(first_ref, second_ref, stat_ref, dkv1_ref, dkv1_out_ref, dkv2_ref, dq_ref):
    _, key1, value1, _ = first_set(first_ref)
    query, key, value, grad = later_set(second_ref)
    log_row = jnp.where(runs(ROWS, 16, 4), MASKED, stat_ref[0:1, :])
    delta_row = stat_ref[1:2, :]
    own_query, own_grad = query[:128], grad[:128]
    probability, score_grad = weigh(own_query, key1, value1, own_grad, log_row[:, :128], delta_row[:, :128])
    dkv1_out_ref[...] = dkv1_ref[...] + key_side(probability, score_grad, own_query, own_grad)
    dq = dot_tn(key1, score_grad)
    probability, score_grad = weigh(query, key, value, grad, log_row, delta_row)
    dkv2_ref[...] = key_side(probability[:128], score_grad[:128], query, grad)
    dq_ref[...] = (dq + dot_tn(key, score_grad[:, :128])) * SCALE


def spread_lanes(value, pick):
    high, low = split2(value)
    return dot_nn(high, pick) + dot_nn(low, pick)


def spread_stats(log_row, delta_row, pick):
    return stat_rows(dot_nn(stat_block(log_row, delta_row).astype(BF), pick))


def level_three(first_ref, second_ref, third_ref, stat1_ref, stat2_ref, out1_ref, out2_ref, dq1_ref, dkv1_ref,
                dq2_ref, dkv2_ref, near_ref, far_ref):
    pick2 = subset_pick(6, 4)
    own_lane = iota((1, 128), 1) < 32

    query, key, value, grad = later_set(third_ref)
    old_log, old_delta = later_stats(third_ref)
    scores, prob_grad, powers, total, new_log, new_delta = set_stats(query, key, value, grad)
    log3, delta3 = merge(old_log, old_delta, new_log, new_delta)
    weight = (jnp.exp(new_log - log3) / total)[:, :128]
    out3 = dot_tn(value, powers[:, :128].astype(BF)) * weight
    own_query, own_grad = query[:128], grad[:128]
    own_log, own_delta = log3[:, :128], delta3[:, :128]

    _, key1, value1, _ = first_set(first_ref)
    octet_log = jnp.where(own_lane, own_log, MASKED)
    probability, score_grad = weigh(own_query, key1, value1, own_grad, octet_log, own_delta)
    dkv1 = dkv1_ref[...] + key_side(probability, score_grad, own_query, own_grad)
    dq = dot_tn(key1, score_grad)
    _, key2, value2, _ = later_set(second_ref)
    probability, score_grad = weigh(own_query, key2, value2, own_grad, own_log, own_delta)
    dkv2 = dkv2_ref[...] + key_side(probability[:128], score_grad[:128], own_query, own_grad)
    dq = dq + dot_tn(key2, score_grad)
    probability = jnp.exp(scores[:, :128] - own_log)
    dq = dq + dot_tn(key, (probability * (prob_grad[:, :128] - own_delta)).astype(BF))
    probability = jnp.exp(scores[:32] - log3)
    score_grad = (probability * (prob_grad[:32] - delta3)).astype(BF)
    dkv3 = key_side(probability.astype(BF), score_grad, query, grad)

    place = iota((128, 1), 0)
    target = lax.shift_left(lax.shift_right_logical(place, 2), 4) + jnp.bitwise_and(place, 3)
    own_pick = one_hot((iota((128, 128), 1) == target) & (place < 32))
    spread_log, spread_delta = spread_stats(own_log, own_delta, own_pick)
    in_third = runs(128, 16, 4)
    log2 = jnp.where(in_third, spread_log, stat2_ref[0:1, :128])
    delta2 = jnp.where(in_third, spread_delta, stat2_ref[1:2, :128])
    merged_t = jnp.where(own_lane, jnp.concatenate([dq * SCALE, out3], axis=0), 0.0)
    fade2 = jnp.exp(stat2_ref[0:1, :128] - log2)
    base_t = jnp.concatenate([dq2_ref[...], out2_ref[...] * fade2], axis=0)
    merged_t = base_t + spread_lanes(merged_t, own_pick)
    high, low = split2(dkv3)
    dkv2 = dkv2 + dot_tn(own_pick[:32], high) + dot_tn(own_pick[:32], low)

    spread_log, spread_delta = spread_stats(log2, delta2, pick2)
    in_second = runs(ROWS, 64, 16)
    log1 = jnp.where(in_second, spread_log, stat1_ref[0:1, :])
    delta1 = jnp.where(in_second, spread_delta, stat1_ref[1:2, :])
    fade1 = jnp.exp(stat1_ref[0:1, :] - log1)
    base_t = jnp.concatenate([dq1_ref[...], out1_ref[...] * fade1], axis=0)
    merged_t = base_t + spread_lanes(merged_t, pick2)
    high, low = split2(dkv2)
    dkv1 = dkv1 + dot_tn(pick2, high) + dot_tn(pick2, low)

    rows = merged_t.T.astype(BF)
    dkv1 = dkv1.astype(BF)
    stats = stat_block(log1, delta1)
    for slot in range(8):
        part = slice(slot * KEPT, (slot + 1) * KEPT)
        target_ref = far_ref if slot % 2 else near_ref
        target_ref[slot // 2, :KEPT, :] = rows[part]
        target_ref[slot // 2, KEPT:2 * KEPT, :] = dkv1[part]
        target_ref[slot // 2, 2 * KEPT:, :] = widen_stats(stats[:, part])


def returned_stats(block):
    return stat_rows(block[2 * KEPT:2 * KEPT + 8, :KEPT])


def kept_attended(info_ref, back_ref, kept_out_ref, kept_log_ref, att_ref):
    for local in range(LOCAL_HEADS):
        block = back_ref[slot_of_head(info_ref, local)]
        log_total, _ = returned_stats(block)
        fade = jnp.exp(kept_log_ref[local:local + 1, :] - log_total)
        fade = jnp.broadcast_to(fade, (HEAD_DIM, KEPT)).T
        sparse = block[:KEPT, 64:].astype(F32)
        att_ref[:, span(local)] = (kept_out_ref[:, span(local)] * fade + sparse).astype(BF)


def tall_pair(half, pair):
    return jnp.concatenate([tall_pick(head_of(half, 2 * pair)), tall_pick(head_of(half, 2 * pair + 1))], axis=1)


def final_grads(info_ref, qkv_ref, packed_ref, kept_grad_ref, back_ref, tall_ref, *rest):
    early, (dq_out_ref, dk_out_ref, dv_out_ref, held, sems) = rest[:9], rest[9:]
    moves = []
    for pair in range(PAIRS):
        back = [back_ref[slot_of_head(info_ref, 2 * pair + spot)] for spot in range(2)]
        key = qkv_ref[1, :, cols(pair)]
        query = diagonal(packed_ref[2 * pair, :KEPT, :64], packed_ref[2 * pair + 1, :KEPT, :64])
        grad = diagonal(kept_grad_ref[:, span(2 * pair)], kept_grad_ref[:, span(2 * pair + 1)])
        stats = [returned_stats(block) for block in back]
        log_total = jnp.concatenate([stat[0] for stat in stats], axis=1)
        delta = jnp.concatenate([stat[1] for stat in stats], axis=1)
        tall = tall_ref[:, cols(pair)]
        probability = jnp.exp(dot_nt(key, query) - log_total)
        score_grad = (probability * (dot_nt(qkv_ref[2, :, cols(pair)], grad) - delta)).astype(BF)
        more_dk = diagonal(*(block[KEPT:2 * KEPT, :64] for block in back))
        more_dv = diagonal(*(block[KEPT:2 * KEPT, 64:] for block in back))
        dk = dot_nn(jnp.concatenate([score_grad, tall], axis=1), jnp.concatenate([query, more_dk], axis=0))
        dv = dot_nn(
            jnp.concatenate([probability.astype(BF), tall], axis=1), jnp.concatenate([grad, more_dv], axis=0)
        )
        crossed = dot_tn(score_grad, key) * SCALE
        more_dq = diagonal(
            crossed[:64, :64] + back[0][:KEPT, :64].astype(F32), crossed[64:, 64:] + back[1][:KEPT, :64].astype(F32)
        )
        dq = dot_nn(jnp.concatenate([tall, tall], axis=1), jnp.concatenate(split2(more_dq), axis=0))
        for which, (more, target) in enumerate(((dq, dq_out_ref), (dk, dk_out_ref), (dv, dv_out_ref))):
            held[pair, which] = (early[3 * pair + which][...] + more).astype(BF)
            move = pltpu.make_async_copy(held.at[pair, which], target.at[:, cols(pair)], sems.at[pair, which])
            move.start()
            moves.append(move)
    for move in moves:
        move.wait()


def mix_base(info_ref, own_att_ref, other_att_ref, own_w_ref, other_w_ref, base_ref, own_tall_ref, other_tall_ref):
    base_ref[...] = dot_tn(own_att_ref[...], own_w_ref[...]) + dot_tn(other_att_ref[...], other_w_ref[...])
    for pair in range(PAIRS):
        own_tall_ref[:, cols(pair)] = tall_pair(info_ref[0], pair)
        other_tall_ref[:, cols(pair)] = tall_pair(1 - info_ref[0], pair)


def spread_kept(tall_ref, kept_ref):
    return jnp.concatenate(
        [
            dot_nn(
                tall_ref[:, cols(pair)], diagonal(kept_ref[:, span(2 * pair)], kept_ref[:, span(2 * pair + 1)])
            ).astype(BF)
            for pair in range(PAIRS)
        ],
        axis=1,
    )


def mix_own(base_ref, kept_ref, tall_ref, w_ref, out_ref):
    out_ref[...] = base_ref[...] + dot_nn(spread_kept(tall_ref, kept_ref), w_ref[...])


def mix_other(base_ref, kept_ref, tall_ref, w_ref, out_ref, held, sems):
    rows = spread_kept(tall_ref, kept_ref)
    moves = []
    for pair in range(PAIRS):
        held[pair] = (base_ref[:, cols(pair)] + dot_nn(rows, w_ref[:, cols(pair)])).astype(BF)
        move = pltpu.make_async_copy(held.at[pair], out_ref.at[:, cols(pair)], sems.at[pair])
        move.start()
        moves.append(move)
    for move in moves:
        move.wait()


def call(kernel, outs, args, flops=0, info=None, after=(), scratch=(), far_out=False):
    shapes = tuple(jax.ShapeDtypeStruct(*out) for out in outs)
    moved = sum(a.size * a.dtype.itemsize for a in args) + sum(
        int(np.prod(shape)) * jnp.dtype(dtype).itemsize for shape, dtype in outs
    )
    scalars = () if info is None else (info,)
    last = len(scalars) + len(args)

    def run(*refs):
        kernel(*refs[:last], *refs[last + len(after):])

    name = getattr(kernel, "func", kernel).__name__
    run.__name__ = name
    near, far = pl.BlockSpec(memory_space=pltpu.VMEM), pl.BlockSpec(memory_space=pltpu.HBM)
    return pl.pallas_call(
        run,
        out_shape=shapes,
        in_specs=[pl.BlockSpec(memory_space=pltpu.SMEM)] * len(scalars)
        + [near] * len(args)
        + [pl.BlockSpec(memory_space=pl.ANY)] * len(after),
        out_specs=(far if far_out else near,) * len(outs),
        scratch_shapes=list(scratch),
        compiler_params=pltpu.CompilerParams(vmem_limit_bytes=VMEM_LIMIT),
        cost_estimate=pl.CostEstimate(flops=flops, bytes_accessed=moved, transcendentals=0),
        name=name,
    )(*scalars, *args, *after)


def partner(array):
    return lax.ppermute(array, "head", [(0, 1), (1, 0)])


def flip(array, mask):
    return lax.ppermute(array, "seq", [(i, i ^ mask) for i in range(lax.axis_size("seq"))])


def gather_pair(array, first, second):
    return jnp.stack([array, flip(array, first), flip(array, second), flip(array, first ^ second)])


def octet_exchange(near, far):
    crossed = flip(far, 1)
    blocks = [jnp.stack([near[chip], crossed[chip]]) for chip in range(4)]
    arrived = {chip: flip(blocks[chip], 2 * chip) for chip in (3, 2, 1)}
    return jnp.concatenate([blocks[0]] + [arrived[chip] for chip in (1, 2, 3)]), blocks[3], arrived[3]


def body(queries, keys, values, weight_out, cotangent):
    half = lax.axis_index("head")
    place = lax.axis_index("seq")
    info = jnp.stack([half, jnp.bitwise_xor(place % 8, 6 * (place // 8 % 2))]).astype(jnp.int32)

    block = ((4, 2 * KEPT + 16, 128), BF)
    later_block = ((272, 128), BF)
    stat = ((8, ROWS), F32)
    square = ((ROWS, WIDE), F32)

    other_cot = partner(cotangent)
    qkv = jnp.stack([queries, keys, values])
    packed, hots = call(
        pack_data, [((LOCAL_HEADS, 2 * KEPT, 128), BF), ((WIDE, ROWS), BF)], (qkv,), flops=200000000, info=info
    )
    kept_out, kept_log = call(
        kept_forward, [((KEPT, WIDE), F32), ((8, KEPT), F32)], (qkv, packed), flops=100000000
    )
    out_t, log0, att_t = call(
        local_forward, [((WIDE, ROWS), F32), stat, ((WIDE, ROWS), BF)], (qkv,), flops=400000000, info=info,
    )
    grad, kept_grad, near, far = call(
        pack_grads, [((ROWS, WIDE), BF), ((KEPT, WIDE), BF), block, block],
        (packed, cotangent, other_cot, weight_out, hots, kept_out, kept_log), flops=400000000, info=info, after=(att_t,),
        scratch=[pltpu.VMEM((8, 2 * KEPT + 16, 128), BF)],
    )
    block1, _, arrived = octet_exchange(near, far)
    late_w, _ = lax.optimization_barrier((weight_out, near))
    late_att, _ = lax.optimization_barrier((att_t, arrived))
    own_w = lax.dynamic_slice_in_dim(late_w, half * WIDE, WIDE, 1)
    mix_w = partner(lax.dynamic_slice_in_dim(late_w, (1 - half) * WIDE, WIDE, 1))
    other_att_t = partner(late_att)

    half_rows = ((128, 128), F32)

    def backward(pair, after):
        return call(
            functools.partial(local_backward, pair), [((ROWS, 128), F32)] * 3, (qkv, grad, log0, out_t),
            flops=300000000, info=info, after=(after,),
        )

    sent2, stat1, out1 = call(
        level_one, [later_block, stat, ((64, ROWS), F32)], (block1,), flops=100000000
    )
    block2 = gather_pair(sent2, 16, 14)
    dq1, dkv1 = call(level_one_back, [((64, ROWS), F32), ((ROWS, 128), F32)], (block1, stat1), flops=100000000)
    early = list(backward(0, sent2))
    sent3, stat2, out2 = call(
        level_two, [later_block, stat, ((64, 128), F32)], (block2,), flops=100000000,
        after=(other_att_t, mix_w, dq1, early[-1]),
    )
    block3 = gather_pair(sent3, 64, 48)
    early.extend(backward(1, sent3))
    dkv1, dkv2, dq2 = call(
        level_two_back, [((ROWS, 128), F32), half_rows, ((64, 128), F32)], (block1, block2, stat2, dkv1),
        flops=100000000,
    )
    base, own_tall, other_tall = call(
        mix_base, [square, ((ROWS, WIDE), BF), ((ROWS, WIDE), BF)],
        (late_att, other_att_t, own_w, mix_w), flops=300000000, info=info,
    )
    near, far = call(
        level_three, [block, block],
        (block1, block2, block3, stat1, stat2, out1, out2, dq1, dkv1, dq2, dkv2), flops=300000000, after=(base, early[-1]),
    )
    back, crossed, _ = octet_exchange(near, far)
    early.extend(backward(2, crossed))
    (own_kept,) = call(
        kept_attended, [((KEPT, WIDE), BF)], (back, kept_out, kept_log), flops=10000000, info=info, after=(early[-1],)
    )
    other_kept = partner(own_kept)
    query_grad, key_grad, value_grad = call(
        final_grads, [((ROWS, WIDE), BF)] * 3, (qkv, packed, kept_grad, back, own_tall, *early),
        flops=200000000, info=info,
        scratch=[pltpu.VMEM((PAIRS, 3, ROWS, 128), BF), pltpu.SemaphoreType.DMA((PAIRS, 3))], far_out=True,
    )
    (nearly,) = call(mix_own, [square], (base, own_kept, own_tall, own_w), flops=200000000)
    (mixed,) = call(
        mix_other, [((ROWS, WIDE), BF)], (nearly, other_kept, other_tall, mix_w), flops=200000000,
        scratch=[pltpu.VMEM((PAIRS, ROWS, 128), BF), pltpu.SemaphoreType.DMA((PAIRS,))], far_out=True,
    )
    return mixed, query_grad, key_grad, value_grad


def solution(mesh):
    specs = P("seq", "head")
    return jax.shard_map(
        body,
        mesh=mesh,
        in_specs=(specs, specs, specs, P("head", None), specs),
        out_specs=(specs, specs, specs, specs),
        check_vma=False,
    )
```

```python
import functools

import jax
import jax.numpy as jnp
import numpy as np
from jax import lax
from jax.experimental import pallas as pl
from jax.experimental.pallas import tpu as pltpu
from jax.sharding import PartitionSpec as P

HEAD_DIM = 64
LOCAL_HEADS = 6
PAIRS = LOCAL_HEADS // 2
ROWS = 512
KEPT = 64
WIDE = 384
SCALE = HEAD_DIM ** -0.5
BF = jnp.bfloat16
F32 = jnp.float32
MASKED = 1e30
VMEM_LIMIT = 24 * 1024 * 1024


def iota(shape, axis):
    return lax.broadcasted_iota(jnp.int32, shape, axis)


def kept_row(place, head):
    phase = lax.shift_right_logical(head, 3)
    third = 16 * place + phase
    later = place - 4
    second = 4 * (later + lax.shift_right_arithmetic(later * 11, 5) + 1) + phase
    last = place - 16
    group = lax.shift_right_arithmetic(last * 171, 9)
    spot = last - 3 * group
    first = 4 * group + spot + jnp.where(spot >= phase, 1, 0)
    chosen = jnp.where(place < 4, third, jnp.where(place < 16, second, first))
    return 8 * chosen + jnp.bitwise_and(head, 7)


def one_hot(match):
    return jnp.where(match, 1.0, 0.0).astype(BF)


def flat_pick(head):
    return one_hot(iota((KEPT, ROWS), 1) == kept_row(iota((KEPT, 1), 0), head))


def tall_pick(head):
    return one_hot(iota((ROWS, KEPT), 0) == kept_row(iota((1, KEPT), 1), head))


def subset_pick(wide, narrow):
    place = iota((128, 1), 0)
    group = lax.shift_right_logical(place, narrow)
    target = lax.shift_left(group, wide) + jnp.bitwise_and(place, (1 << narrow) - 1)
    return one_hot(iota((128, ROWS), 1) == target)


def dot_nn(left, right):
    return lax.dot_general(left, right, (((1,), (0,)), ((), ())), preferred_element_type=F32)


def dot_nt(left, right):
    return lax.dot_general(left, right, (((1,), (1,)), ((), ())), preferred_element_type=F32)


def dot_tn(left, right):
    return lax.dot_general(left, right, (((0,), (0,)), ((), ())), preferred_element_type=F32)


def split2(value):
    high = value.astype(BF)
    return high, (value - high.astype(F32)).astype(BF)


def split3(value):
    high = value.astype(BF)
    rest = value - high.astype(F32)
    middle = rest.astype(BF)
    return high, middle, (rest - middle.astype(F32)).astype(BF)


def stat_block(log_row, delta_row):
    pieces = split3(log_row) + split3(delta_row)
    rows = [piece.astype(F32) for piece in pieces]
    zero = jnp.zeros_like(log_row)
    return jnp.concatenate(rows + [zero, zero], axis=0)


def stat_rows(block):
    block = block.astype(F32)
    log_row = block[0:1] + block[1:2] + block[2:3]
    delta_row = block[3:4] + block[4:5] + block[5:6]
    return log_row, delta_row


def log_add(first, second):
    peak = jnp.maximum(first, second)
    return peak + jnp.log(jnp.exp(first - peak) + jnp.exp(second - peak))


def span(local):
    return slice(local * HEAD_DIM, (local + 1) * HEAD_DIM)


def cols(pair):
    return slice(pair * 128, (pair + 1) * 128)


OWNERS = (0, 2, 4, 3, 5, 7)
IDLE = (1, 6)


def slot_of(info_ref, place):
    return jnp.bitwise_xor(info_ref[1], place)


def slot_of_head(info_ref, local):
    return slot_of(info_ref, OWNERS[local])


def head_of(half, local):
    return half * LOCAL_HEADS + local


def diagonal(first, second):
    zero = jnp.zeros_like(first)
    return jnp.concatenate(
        [jnp.concatenate([first, zero], axis=1), jnp.concatenate([zero, second], axis=1)], axis=0
    )


def pack_data(info_ref, qkv_ref, packed_ref, hots_ref):
    for local in range(LOCAL_HEADS):
        hot = flat_pick(head_of(info_ref[0], local))
        hots_ref[span(local), :] = hot
        joined = jnp.concatenate([qkv_ref[part, :, span(local)] for part in range(3)], axis=1)
        rows = dot_nn(hot, joined).astype(BF)
        packed_ref[local, :KEPT, :] = jnp.concatenate([rows[:, :64] * BF(SCALE), rows[:, 64:128]], axis=1)
        packed_ref[local, KEPT:, :] = jnp.concatenate([rows[:, 128:], jnp.zeros((KEPT, 64), BF)], axis=1)


def kept_forward(qkv_ref, packed_ref, out_ref, log_ref):
    log_ref[LOCAL_HEADS:, :] = jnp.zeros((8 - LOCAL_HEADS, KEPT), F32)
    for pair in range(PAIRS):
        query = diagonal(packed_ref[2 * pair, :KEPT, :64], packed_ref[2 * pair + 1, :KEPT, :64])
        scores = dot_nt(qkv_ref[1, :, cols(pair)], query)
        peak = jnp.max(scores, axis=0, keepdims=True)
        powers = jnp.exp(scores - peak)
        total = jnp.sum(powers, axis=0, keepdims=True)
        crossed = (dot_tn(qkv_ref[2, :, cols(pair)], powers.astype(BF)) / total).T
        out_ref[:, cols(pair)] = jnp.concatenate([crossed[:64, :64], crossed[64:, 64:]], axis=1)
        log_row = peak + jnp.log(total)
        log_ref[2 * pair:2 * pair + 1, :] = log_row[:, :64]
        log_ref[2 * pair + 1:2 * pair + 2, :] = log_row[:, 64:]


def own_grads(info_ref, own_cot_ref, w_ref, out_ref):
    own_w = w_ref[:, pl.ds(pl.multiple_of(info_ref[0] * WIDE, 128), WIDE)]
    out_ref[...] = dot_nt(own_cot_ref[...], own_w)


def pack_grads(info_ref, packed_ref, own_part_ref, other_cot_ref, w_ref, hots_ref, kept_out_ref,
               kept_log_ref, grad_ref, kept_grad_ref, near_ref, far_ref, slots):
    other_w = w_ref[:, pl.ds(pl.multiple_of((1 - info_ref[0]) * WIDE, 128), WIDE)]
    grad = (own_part_ref[...] + dot_nt(other_cot_ref[...], other_w)).astype(BF)
    grad_ref[...] = grad
    for local in range(LOCAL_HEADS):
        rows = dot_nn(hots_ref[span(local), :], grad[:, span(local)])
        kept_grad = rows.astype(BF)
        kept_grad_ref[:, span(local)] = kept_grad
        delta = jnp.sum((rows * kept_out_ref[:, span(local)]).T, axis=0, keepdims=True)
        slot = slot_of_head(info_ref, local)
        slots[slot, :KEPT, :] = packed_ref[local, :KEPT, :]
        slots[slot, KEPT:2 * KEPT, :] = jnp.concatenate([packed_ref[local, KEPT:, :64], kept_grad], axis=1)
        slots[slot, 2 * KEPT:, :] = widen_stats(stat_block(kept_log_ref[local:local + 1, :], delta))
    for spare in IDLE:
        slots[slot_of(info_ref, spare)] = jnp.zeros((2 * KEPT + 16, 128), BF)
    for chip in range(4):
        near_ref[chip] = slots[2 * chip]
        far_ref[chip] = slots[2 * chip + 1]


def local_forward(info_ref, qkv_ref, out_t_ref, log_ref, att_t_ref):
    log_ref[LOCAL_HEADS:, :] = jnp.zeros((8 - LOCAL_HEADS, ROWS), F32)
    for local in range(LOCAL_HEADS):
        scores = dot_nt(qkv_ref[1, :, span(local)], qkv_ref[0, :, span(local)] * BF(SCALE))
        peak = jnp.max(scores, axis=0, keepdims=True)
        powers = jnp.exp(scores - peak)
        total = jnp.sum(powers, axis=0, keepdims=True)
        out_t = dot_tn(qkv_ref[2, :, span(local)], powers.astype(BF)) / total
        log_row = peak + jnp.log(total)
        out_t_ref[span(local), :] = out_t
        log_ref[local:local + 1, :] = log_row
        head = head_of(info_ref[0], local)
        is_kept = jnp.bitwise_and(iota((1, ROWS), 1), 7) == jnp.bitwise_and(head, 7)
        att_t_ref[span(local), :] = jnp.where(is_kept, 0.0, out_t).astype(BF)


def widen_stats(block):
    if block.shape[1] < 128:
        block = jnp.concatenate([block, jnp.zeros((8, 128 - block.shape[1]), F32)], axis=1)
    return jnp.concatenate([block, jnp.zeros((8, 128), F32)], axis=0).astype(BF)


def local_backward(pair, info_ref, qkv_ref, grad_ref, log_ref, out_t_ref, dq_ref, dk_ref, dv_ref):
    dq_t, dk, dv = [], [], []
    for local in (2 * pair, 2 * pair + 1):
        query = qkv_ref[0, :, span(local)] * BF(SCALE)
        key = qkv_ref[1, :, span(local)]
        grad = grad_ref[:, span(local)]
        head = head_of(info_ref[0], local)
        is_kept = jnp.bitwise_and(iota((1, ROWS), 1), 7) == jnp.bitwise_and(head, 7)
        log_row = jnp.where(is_kept, MASKED, log_ref[local:local + 1, :])
        probability = jnp.exp(dot_nt(key, query) - log_row)
        delta = jnp.sum(grad.astype(F32).T * out_t_ref[span(local), :], axis=0, keepdims=True)
        score_grad = probability * (dot_nt(qkv_ref[2, :, span(local)], grad) - delta)
        score_grad = score_grad.astype(BF)
        dv.append(dot_nn(probability.astype(BF), grad))
        dk.append(dot_nn(score_grad, query))
        dq_t.append(dot_tn(key, score_grad))
    dq_ref[...] = jnp.concatenate(dq_t, axis=0).T * SCALE
    dk_ref[...] = jnp.concatenate(dk, axis=1)
    dv_ref[...] = jnp.concatenate(dv, axis=1)


def set_stats(query, key, value, grad):
    scores = dot_nt(key, query)
    peak = jnp.max(scores, axis=0, keepdims=True)
    powers = jnp.exp(scores - peak)
    total = jnp.sum(powers, axis=0, keepdims=True)
    prob_grad = dot_nt(value, grad)
    delta = jnp.sum(powers * prob_grad, axis=0, keepdims=True) / total
    return scores, prob_grad, powers, total, peak + jnp.log(total), delta


def merge(old_log, old_delta, new_log, new_delta):
    joint = log_add(old_log, new_log)
    return joint, jnp.exp(old_log - joint) * old_delta + jnp.exp(new_log - joint) * new_delta


def first_set(block_ref):
    joined = block_ref[:, :KEPT, :].reshape(ROWS, 128)
    other = block_ref[:, KEPT:2 * KEPT, :].reshape(ROWS, 128)
    return joined[:, :64], joined[:, 64:], other[:, :64], other[:, 64:]


def later_set(block_ref):
    joined = block_ref[:, :128, :].reshape(ROWS, 128)
    other = block_ref[:, 128:256, :].reshape(ROWS, 128)
    return joined[:, :64], joined[:, 64:], other[:, :64], other[:, 64:]


def later_stats(block_ref):
    return stat_rows(jnp.concatenate([block_ref[i, 256:264, :].astype(F32) for i in range(4)], axis=1))


def level_one(block_ref, payload_ref, stat_ref, out_t_ref):
    query, key, value, grad = first_set(block_ref)
    stats = jnp.concatenate([block_ref[i, 128:136, :KEPT].astype(F32) for i in range(8)], axis=1)
    old_log, old_delta = stat_rows(stats)
    _, _, powers, total, new_log, new_delta = set_stats(query, key, value, grad)
    joint, delta = merge(old_log, old_delta, new_log, new_delta)
    out_t_ref[...] = dot_tn(value, powers.astype(BF)) * (jnp.exp(new_log - joint) / total)
    stat_ref[0:1, :] = joint
    stat_ref[1:2, :] = delta
    stat_ref[2:, :] = jnp.zeros((6, ROWS), F32)
    payload_ref[:128, :] = block_ref[:, :16, :].reshape(128, 128)
    payload_ref[128:256, :] = block_ref[:, KEPT:KEPT + 16, :].reshape(128, 128)
    picked = dot_nt(stat_block(joint, delta).astype(BF), subset_pick(6, 4))
    payload_ref[256:, :] = widen_stats(picked)


def level_two(block_ref, payload_ref, stat_ref, out_t_ref):
    pick = subset_pick(4, 2)
    query, key, value, grad = later_set(block_ref)
    old_log, old_delta = later_stats(block_ref)
    _, _, powers, total, new_log, new_delta = set_stats(query, key, value, grad)
    joint, delta = merge(old_log, old_delta, new_log, new_delta)
    weight = (jnp.exp(new_log - joint) / total)[:, :128]
    out_t_ref[...] = dot_tn(value, powers[:, :128].astype(BF)) * weight
    stat_ref[0:1, :] = joint
    stat_ref[1:2, :] = delta
    stat_ref[2:, :] = jnp.zeros((6, ROWS), F32)
    payload_ref[:128, :] = dot_nn(pick, block_ref[:, :128, :].reshape(ROWS, 128)).astype(BF)
    payload_ref[128:256, :] = dot_nn(pick, block_ref[:, 128:256, :].reshape(ROWS, 128)).astype(BF)
    picked = dot_nt(stat_block(joint, delta).astype(BF), pick)
    payload_ref[256:, :] = widen_stats(picked)


def weigh(query, key, value, grad, log_row, delta_row):
    probability = jnp.exp(dot_nt(key, query) - log_row)
    score_grad = probability * (dot_nt(value, grad) - delta_row)
    return probability.astype(BF), score_grad.astype(BF)


def key_side(probability, score_grad, query, grad):
    return jnp.concatenate([dot_nn(score_grad, query), dot_nn(probability, grad)], axis=1)


def runs(lanes, wide, narrow):
    return jnp.bitwise_and(iota((1, lanes), 1), wide - 1) < narrow


def level_one_back(block_ref, stat_ref, dq_ref, dkv_ref):
    query, key, value, grad = first_set(block_ref)
    log_row = jnp.where(runs(ROWS, 64, 16), MASKED, stat_ref[0:1, :])
    probability, score_grad = weigh(query, key, value, grad, log_row, stat_ref[1:2, :])
    dq_ref[...] = dot_tn(key, score_grad) * SCALE
    dkv_ref[...] = key_side(probability, score_grad, query, grad)


def level_two_back(first_ref, second_ref, stat_ref, dkv1_ref, dkv1_out_ref, dkv2_ref, dq_ref):
    _, key1, value1, _ = first_set(first_ref)
    query, key, value, grad = later_set(second_ref)
    log_row = jnp.where(runs(ROWS, 16, 4), MASKED, stat_ref[0:1, :])
    delta_row = stat_ref[1:2, :]
    own_query, own_grad = query[:128], grad[:128]
    probability, score_grad = weigh(own_query, key1, value1, own_grad, log_row[:, :128], delta_row[:, :128])
    dkv1_out_ref[...] = dkv1_ref[...] + key_side(probability, score_grad, own_query, own_grad)
    dq = dot_tn(key1, score_grad)
    probability, score_grad = weigh(query, key, value, grad, log_row, delta_row)
    dkv2_ref[...] = key_side(probability[:128], score_grad[:128], query, grad)
    dq_ref[...] = (dq + dot_tn(key, score_grad[:, :128])) * SCALE


def spread_lanes(value, pick):
    high, low = split2(value)
    return dot_nn(high, pick) + dot_nn(low, pick)


def spread_stats(log_row, delta_row, pick):
    return stat_rows(dot_nn(stat_block(log_row, delta_row).astype(BF), pick))


def level_three(first_ref, second_ref, third_ref, stat1_ref, stat2_ref, out1_ref, out2_ref, dq1_ref, dkv1_ref,
                dq2_ref, dkv2_ref, near_ref, far_ref):
    pick2 = subset_pick(6, 4)
    own_lane = iota((1, 128), 1) < 32

    query, key, value, grad = later_set(third_ref)
    old_log, old_delta = later_stats(third_ref)
    scores, prob_grad, powers, total, new_log, new_delta = set_stats(query, key, value, grad)
    log3, delta3 = merge(old_log, old_delta, new_log, new_delta)
    weight = (jnp.exp(new_log - log3) / total)[:, :128]
    out3 = dot_tn(value, powers[:, :128].astype(BF)) * weight
    own_query, own_grad = query[:128], grad[:128]
    own_log, own_delta = log3[:, :128], delta3[:, :128]

    _, key1, value1, _ = first_set(first_ref)
    octet_log = jnp.where(own_lane, own_log, MASKED)
    probability, score_grad = weigh(own_query, key1, value1, own_grad, octet_log, own_delta)
    dkv1 = dkv1_ref[...] + key_side(probability, score_grad, own_query, own_grad)
    dq = dot_tn(key1, score_grad)
    _, key2, value2, _ = later_set(second_ref)
    probability, score_grad = weigh(own_query, key2, value2, own_grad, own_log, own_delta)
    dkv2 = dkv2_ref[...] + key_side(probability[:128], score_grad[:128], own_query, own_grad)
    dq = dq + dot_tn(key2, score_grad)
    probability = jnp.exp(scores[:, :128] - own_log)
    dq = dq + dot_tn(key, (probability * (prob_grad[:, :128] - own_delta)).astype(BF))
    probability = jnp.exp(scores[:32] - log3)
    score_grad = (probability * (prob_grad[:32] - delta3)).astype(BF)
    dkv3 = key_side(probability.astype(BF), score_grad, query, grad)

    place = iota((128, 1), 0)
    target = lax.shift_left(lax.shift_right_logical(place, 2), 4) + jnp.bitwise_and(place, 3)
    own_pick = one_hot((iota((128, 128), 1) == target) & (place < 32))
    spread_log, spread_delta = spread_stats(own_log, own_delta, own_pick)
    in_third = runs(128, 16, 4)
    log2 = jnp.where(in_third, spread_log, stat2_ref[0:1, :128])
    delta2 = jnp.where(in_third, spread_delta, stat2_ref[1:2, :128])
    merged_t = jnp.where(own_lane, jnp.concatenate([dq * SCALE, out3], axis=0), 0.0)
    fade2 = jnp.exp(stat2_ref[0:1, :128] - log2)
    base_t = jnp.concatenate([dq2_ref[...], out2_ref[...] * fade2], axis=0)
    merged_t = base_t + spread_lanes(merged_t, own_pick)
    high, low = split2(dkv3)
    dkv2 = dkv2 + dot_tn(own_pick[:32], high) + dot_tn(own_pick[:32], low)

    spread_log, spread_delta = spread_stats(log2, delta2, pick2)
    in_second = runs(ROWS, 64, 16)
    log1 = jnp.where(in_second, spread_log, stat1_ref[0:1, :])
    delta1 = jnp.where(in_second, spread_delta, stat1_ref[1:2, :])
    fade1 = jnp.exp(stat1_ref[0:1, :] - log1)
    base_t = jnp.concatenate([dq1_ref[...], out1_ref[...] * fade1], axis=0)
    merged_t = base_t + spread_lanes(merged_t, pick2)
    high, low = split2(dkv2)
    dkv1 = dkv1 + dot_tn(pick2, high) + dot_tn(pick2, low)

    rows = merged_t.T.astype(BF)
    dkv1 = dkv1.astype(BF)
    stats = stat_block(log1, delta1)
    for slot in range(8):
        part = slice(slot * KEPT, (slot + 1) * KEPT)
        target_ref = far_ref if slot % 2 else near_ref
        target_ref[slot // 2, :KEPT, :] = rows[part]
        target_ref[slot // 2, KEPT:2 * KEPT, :] = dkv1[part]
        target_ref[slot // 2, 2 * KEPT:, :] = widen_stats(stats[:, part])


def returned_stats(block):
    return stat_rows(block[2 * KEPT:2 * KEPT + 8, :KEPT])


def kept_attended(info_ref, back_ref, kept_out_ref, kept_log_ref, att_ref):
    for local in range(LOCAL_HEADS):
        block = back_ref[slot_of_head(info_ref, local)]
        log_total, _ = returned_stats(block)
        fade = jnp.exp(kept_log_ref[local:local + 1, :] - log_total)
        fade = jnp.broadcast_to(fade, (HEAD_DIM, KEPT)).T
        sparse = block[:KEPT, 64:].astype(F32)
        att_ref[:, span(local)] = (kept_out_ref[:, span(local)] * fade + sparse).astype(BF)


def tall_pair(half, pair):
    return jnp.concatenate([tall_pick(head_of(half, 2 * pair)), tall_pick(head_of(half, 2 * pair + 1))], axis=1)


def final_grads(info_ref, qkv_ref, packed_ref, kept_grad_ref, back_ref, tall_ref, *rest):
    early, (dq_out_ref, dk_out_ref, dv_out_ref, held, sems) = rest[:9], rest[9:]
    moves = []
    for pair in range(PAIRS):
        back = [back_ref[slot_of_head(info_ref, 2 * pair + spot)] for spot in range(2)]
        key = qkv_ref[1, :, cols(pair)]
        query = diagonal(packed_ref[2 * pair, :KEPT, :64], packed_ref[2 * pair + 1, :KEPT, :64])
        grad = diagonal(kept_grad_ref[:, span(2 * pair)], kept_grad_ref[:, span(2 * pair + 1)])
        stats = [returned_stats(block) for block in back]
        log_total = jnp.concatenate([stat[0] for stat in stats], axis=1)
        delta = jnp.concatenate([stat[1] for stat in stats], axis=1)
        tall = tall_ref[:, cols(pair)]
        probability = jnp.exp(dot_nt(key, query) - log_total)
        score_grad = (probability * (dot_nt(qkv_ref[2, :, cols(pair)], grad) - delta)).astype(BF)
        more_dk = diagonal(*(block[KEPT:2 * KEPT, :64] for block in back))
        more_dv = diagonal(*(block[KEPT:2 * KEPT, 64:] for block in back))
        dk = dot_nn(jnp.concatenate([score_grad, tall], axis=1), jnp.concatenate([query, more_dk], axis=0))
        dv = dot_nn(
            jnp.concatenate([probability.astype(BF), tall], axis=1), jnp.concatenate([grad, more_dv], axis=0)
        )
        crossed = dot_tn(score_grad, key) * SCALE
        more_dq = diagonal(
            crossed[:64, :64] + back[0][:KEPT, :64].astype(F32), crossed[64:, 64:] + back[1][:KEPT, :64].astype(F32)
        )
        dq = dot_nn(jnp.concatenate([tall, tall], axis=1), jnp.concatenate(split2(more_dq), axis=0))
        for which, (more, target) in enumerate(((dq, dq_out_ref), (dk, dk_out_ref), (dv, dv_out_ref))):
            held[pair, which] = (early[3 * pair + which][...] + more).astype(BF)
            move = pltpu.make_async_copy(held.at[pair, which], target.at[:, cols(pair)], sems.at[pair, which])
            move.start()
            moves.append(move)
    for move in moves:
        move.wait()


def mix_base(info_ref, own_att_ref, other_att_ref, own_w_ref, other_w_ref, base_ref, own_tall_ref, other_tall_ref):
    base_ref[...] = dot_tn(own_att_ref[...], own_w_ref[...]) + dot_tn(other_att_ref[...], other_w_ref[...])
    for pair in range(PAIRS):
        own_tall_ref[:, cols(pair)] = tall_pair(info_ref[0], pair)
        other_tall_ref[:, cols(pair)] = tall_pair(1 - info_ref[0], pair)


def spread_kept(tall_ref, kept_ref):
    return jnp.concatenate(
        [
            dot_nn(
                tall_ref[:, cols(pair)], diagonal(kept_ref[:, span(2 * pair)], kept_ref[:, span(2 * pair + 1)])
            ).astype(BF)
            for pair in range(PAIRS)
        ],
        axis=1,
    )


def mix_own(base_ref, kept_ref, tall_ref, w_ref, out_ref):
    out_ref[...] = base_ref[...] + dot_nn(spread_kept(tall_ref, kept_ref), w_ref[...])


def mix_other(base_ref, kept_ref, tall_ref, w_ref, out_ref, held, sems):
    rows = spread_kept(tall_ref, kept_ref)
    moves = []
    for pair in range(PAIRS):
        held[pair] = (base_ref[:, cols(pair)] + dot_nn(rows, w_ref[:, cols(pair)])).astype(BF)
        move = pltpu.make_async_copy(held.at[pair], out_ref.at[:, cols(pair)], sems.at[pair])
        move.start()
        moves.append(move)
    for move in moves:
        move.wait()


def call(kernel, outs, args, flops=0, info=None, after=(), scratch=(), far_out=False):
    shapes = tuple(jax.ShapeDtypeStruct(*out) for out in outs)
    moved = sum(a.size * a.dtype.itemsize for a in args) + sum(
        int(np.prod(shape)) * jnp.dtype(dtype).itemsize for shape, dtype in outs
    )
    scalars = () if info is None else (info,)
    last = len(scalars) + len(args)

    def run(*refs):
        kernel(*refs[:last], *refs[last + len(after):])

    name = getattr(kernel, "func", kernel).__name__
    run.__name__ = name
    near, far = pl.BlockSpec(memory_space=pltpu.VMEM), pl.BlockSpec(memory_space=pltpu.HBM)
    return pl.pallas_call(
        run,
        out_shape=shapes,
        in_specs=[pl.BlockSpec(memory_space=pltpu.SMEM)] * len(scalars)
        + [near] * len(args)
        + [pl.BlockSpec(memory_space=pl.ANY)] * len(after),
        out_specs=(far if far_out else near,) * len(outs),
        scratch_shapes=list(scratch),
        compiler_params=pltpu.CompilerParams(vmem_limit_bytes=VMEM_LIMIT),
        cost_estimate=pl.CostEstimate(flops=flops, bytes_accessed=moved, transcendentals=0),
        name=name,
    )(*scalars, *args, *after)


def partner(array):
    return lax.ppermute(array, "head", [(0, 1), (1, 0)])


def flip(array, mask):
    return lax.ppermute(array, "seq", [(i, i ^ mask) for i in range(lax.axis_size("seq"))])


def gather_pair(array, first, second):
    return jnp.stack([array, flip(array, first), flip(array, second), flip(array, first ^ second)])


def octet_exchange(near, far, order):
    crossed = flip(far, 1)
    blocks = [jnp.stack([near[chip], crossed[chip]]) for chip in range(4)]
    arrived = {chip: flip(blocks[chip], 2 * chip) for chip in order}
    return jnp.concatenate([blocks[0]] + [arrived[chip] for chip in (1, 2, 3)]), blocks[3], arrived[order[0]]


def body(queries, keys, values, weight_out, cotangent):
    half = lax.axis_index("head")
    place = lax.axis_index("seq")
    info = jnp.stack([half, jnp.bitwise_xor(place % 8, 6 * (place // 8 % 2))]).astype(jnp.int32)

    block = ((4, 2 * KEPT + 16, 128), BF)
    later_block = ((272, 128), BF)
    stat = ((8, ROWS), F32)
    square = ((ROWS, WIDE), F32)

    other_cot = partner(cotangent)
    qkv = jnp.stack([queries, keys, values])
    packed, hots = call(
        pack_data, [((LOCAL_HEADS, 2 * KEPT, 128), BF), ((WIDE, ROWS), BF)], (qkv,), flops=200000000, info=info
    )
    kept_out, kept_log = call(
        kept_forward, [((KEPT, WIDE), F32), ((8, KEPT), F32)], (qkv, packed), flops=100000000
    )
    out_t, log0, att_t = call(
        local_forward, [((WIDE, ROWS), F32), stat, ((WIDE, ROWS), BF)], (qkv,), flops=400000000, info=info,
    )
    (own_part,) = call(own_grads, [square], (cotangent, weight_out), flops=200000000, info=info)
    grad, kept_grad, near, far = call(
        pack_grads, [((ROWS, WIDE), BF), ((KEPT, WIDE), BF), block, block],
        (packed, own_part, other_cot, weight_out, hots, kept_out, kept_log), flops=400000000, info=info, after=(att_t,),
        scratch=[pltpu.VMEM((8, 2 * KEPT + 16, 128), BF)],
    )
    block1, _, arrived = octet_exchange(near, far, (3, 2, 1))
    late_w, _ = lax.optimization_barrier((weight_out, near))
    late_att, _ = lax.optimization_barrier((att_t, arrived))
    own_w = lax.dynamic_slice_in_dim(late_w, half * WIDE, WIDE, 1)
    mix_w = partner(lax.dynamic_slice_in_dim(late_w, (1 - half) * WIDE, WIDE, 1))
    other_att_t = partner(late_att)

    half_rows = ((128, 128), F32)

    def backward(pair, after):
        return call(
            functools.partial(local_backward, pair), [((ROWS, 128), F32)] * 3, (qkv, grad, log0, out_t),
            flops=300000000, info=info, after=(after,),
        )

    sent2, stat1, out1 = call(
        level_one, [later_block, stat, ((64, ROWS), F32)], (block1,), flops=100000000
    )
    block2 = gather_pair(sent2, 16, 14)
    dq1, dkv1 = call(level_one_back, [((64, ROWS), F32), ((ROWS, 128), F32)], (block1, stat1), flops=100000000)
    early = list(backward(0, sent2))
    sent3, stat2, out2 = call(
        level_two, [later_block, stat, ((64, 128), F32)], (block2,), flops=100000000,
        after=(other_att_t, mix_w, dq1, early[-1]),
    )
    block3 = gather_pair(sent3, 64, 48)
    early.extend(backward(1, sent3))
    dkv1, dkv2, dq2 = call(
        level_two_back, [((ROWS, 128), F32), half_rows, ((64, 128), F32)], (block1, block2, stat2, dkv1),
        flops=100000000,
    )
    base, own_tall, other_tall = call(
        mix_base, [square, ((ROWS, WIDE), BF), ((ROWS, WIDE), BF)],
        (late_att, other_att_t, own_w, mix_w), flops=300000000, info=info,
    )
    near, far = call(
        level_three, [block, block],
        (block1, block2, block3, stat1, stat2, out1, out2, dq1, dkv1, dq2, dkv2), flops=300000000, after=(base, early[-1]),
    )
    back, crossed, _ = octet_exchange(near, far, (2, 3, 1))
    early.extend(backward(2, crossed))
    (own_kept,) = call(
        kept_attended, [((KEPT, WIDE), BF)], (back, kept_out, kept_log), flops=10000000, info=info, after=(early[-1],)
    )
    other_kept = partner(own_kept)
    query_grad, key_grad, value_grad = call(
        final_grads, [((ROWS, WIDE), BF)] * 3, (qkv, packed, kept_grad, back, own_tall, *early),
        flops=200000000, info=info,
        scratch=[pltpu.VMEM((PAIRS, 3, ROWS, 128), BF), pltpu.SemaphoreType.DMA((PAIRS, 3))], far_out=True,
    )
    (nearly,) = call(mix_own, [square], (base, own_kept, own_tall, own_w), flops=200000000)
    (mixed,) = call(
        mix_other, [((ROWS, WIDE), BF)], (nearly, other_kept, other_tall, mix_w), flops=200000000,
        scratch=[pltpu.VMEM((PAIRS, ROWS, 128), BF), pltpu.SemaphoreType.DMA((PAIRS,))], far_out=True,
    )
    return mixed, query_grad, key_grad, value_grad


def solution(mesh):
    specs = P("seq", "head")
    return jax.shard_map(
        body,
        mesh=mesh,
        in_specs=(specs, specs, specs, P("head", None), specs),
        out_specs=(specs, specs, specs, specs),
        check_vma=False,
    )
```

```python
import functools

import jax
import jax.numpy as jnp
import numpy as np
from jax import lax
from jax.experimental import pallas as pl
from jax.experimental.pallas import tpu as pltpu
from jax.sharding import PartitionSpec as P

HEAD_DIM = 64
LOCAL_HEADS = 6
PAIRS = LOCAL_HEADS // 2
ROWS = 512
KEPT = 64
WIDE = 384
SCALE = HEAD_DIM ** -0.5
BF = jnp.bfloat16
F32 = jnp.float32
MASKED = 1e30
VMEM_LIMIT = 24 * 1024 * 1024


def iota(shape, axis):
    return lax.broadcasted_iota(jnp.int32, shape, axis)


def kept_row(place, head):
    phase = lax.shift_right_logical(head, 3)
    third = 16 * place + phase
    later = place - 4
    second = 4 * (later + lax.shift_right_arithmetic(later * 11, 5) + 1) + phase
    last = place - 16
    group = lax.shift_right_arithmetic(last * 171, 9)
    spot = last - 3 * group
    first = 4 * group + spot + jnp.where(spot >= phase, 1, 0)
    chosen = jnp.where(place < 4, third, jnp.where(place < 16, second, first))
    return 8 * chosen + jnp.bitwise_and(head, 7)


def one_hot(match):
    return jnp.where(match, 1.0, 0.0).astype(BF)


def flat_pick(head):
    return one_hot(iota((KEPT, ROWS), 1) == kept_row(iota((KEPT, 1), 0), head))


def tall_pick(head):
    return one_hot(iota((ROWS, KEPT), 0) == kept_row(iota((1, KEPT), 1), head))


def subset_pick(wide, narrow):
    place = iota((128, 1), 0)
    group = lax.shift_right_logical(place, narrow)
    target = lax.shift_left(group, wide) + jnp.bitwise_and(place, (1 << narrow) - 1)
    return one_hot(iota((128, ROWS), 1) == target)


def dot_nn(left, right):
    return lax.dot_general(left, right, (((1,), (0,)), ((), ())), preferred_element_type=F32)


def dot_nt(left, right):
    return lax.dot_general(left, right, (((1,), (1,)), ((), ())), preferred_element_type=F32)


def dot_tn(left, right):
    return lax.dot_general(left, right, (((0,), (0,)), ((), ())), preferred_element_type=F32)


def split2(value):
    high = value.astype(BF)
    return high, (value - high.astype(F32)).astype(BF)


def split3(value):
    high = value.astype(BF)
    rest = value - high.astype(F32)
    middle = rest.astype(BF)
    return high, middle, (rest - middle.astype(F32)).astype(BF)


def stat_block(log_row, delta_row):
    pieces = split3(log_row) + split3(delta_row)
    rows = [piece.astype(F32) for piece in pieces]
    zero = jnp.zeros_like(log_row)
    return jnp.concatenate(rows + [zero, zero], axis=0)


def stat_rows(block):
    block = block.astype(F32)
    log_row = block[0:1] + block[1:2] + block[2:3]
    delta_row = block[3:4] + block[4:5] + block[5:6]
    return log_row, delta_row


def log_add(first, second):
    peak = jnp.maximum(first, second)
    return peak + jnp.log(jnp.exp(first - peak) + jnp.exp(second - peak))


def span(local):
    return slice(local * HEAD_DIM, (local + 1) * HEAD_DIM)


def cols(pair):
    return slice(pair * 128, (pair + 1) * 128)


OWNERS = (0, 2, 4, 3, 5, 7)
IDLE = (1, 6)


def slot_of(info_ref, place):
    return jnp.bitwise_xor(info_ref[1], place)


def slot_of_head(info_ref, local):
    return slot_of(info_ref, OWNERS[local])


def head_of(half, local):
    return half * LOCAL_HEADS + local


def diagonal(first, second):
    zero = jnp.zeros_like(first)
    return jnp.concatenate(
        [jnp.concatenate([first, zero], axis=1), jnp.concatenate([zero, second], axis=1)], axis=0
    )


def pack_data(info_ref, qkv_ref, packed_ref, hots_ref):
    for local in range(LOCAL_HEADS):
        hot = flat_pick(head_of(info_ref[0], local))
        hots_ref[span(local), :] = hot
        joined = jnp.concatenate([qkv_ref[part, :, span(local)] for part in range(3)], axis=1)
        rows = dot_nn(hot, joined).astype(BF)
        packed_ref[local, :KEPT, :] = jnp.concatenate([rows[:, :64] * BF(SCALE), rows[:, 64:128]], axis=1)
        packed_ref[local, KEPT:, :] = jnp.concatenate([rows[:, 128:], jnp.zeros((KEPT, 64), BF)], axis=1)


def kept_forward(qkv_ref, packed_ref, out_ref, log_ref):
    log_ref[LOCAL_HEADS:, :] = jnp.zeros((8 - LOCAL_HEADS, KEPT), F32)
    for pair in range(PAIRS):
        query = diagonal(packed_ref[2 * pair, :KEPT, :64], packed_ref[2 * pair + 1, :KEPT, :64])
        scores = dot_nt(qkv_ref[1, :, cols(pair)], query)
        peak = jnp.max(scores, axis=0, keepdims=True)
        powers = jnp.exp(scores - peak)
        total = jnp.sum(powers, axis=0, keepdims=True)
        crossed = (dot_tn(qkv_ref[2, :, cols(pair)], powers.astype(BF)) / total).T
        out_ref[:, cols(pair)] = jnp.concatenate([crossed[:64, :64], crossed[64:, 64:]], axis=1)
        log_row = peak + jnp.log(total)
        log_ref[2 * pair:2 * pair + 1, :] = log_row[:, :64]
        log_ref[2 * pair + 1:2 * pair + 2, :] = log_row[:, 64:]


def pack_grads(info_ref, packed_ref, own_cot_ref, other_cot_ref, w_ref, hots_ref, kept_out_ref,
               kept_log_ref, grad_ref, kept_grad_ref, near_ref, far_ref, slots):
    own_w = w_ref[:, pl.ds(pl.multiple_of(info_ref[0] * WIDE, 128), WIDE)]
    other_w = w_ref[:, pl.ds(pl.multiple_of((1 - info_ref[0]) * WIDE, 128), WIDE)]
    grad = (dot_nt(own_cot_ref[...], own_w) + dot_nt(other_cot_ref[...], other_w)).astype(BF)
    grad_ref[...] = grad
    for local in range(LOCAL_HEADS):
        rows = dot_nn(hots_ref[span(local), :], grad[:, span(local)])
        kept_grad = rows.astype(BF)
        kept_grad_ref[:, span(local)] = kept_grad
        delta = jnp.sum((rows * kept_out_ref[:, span(local)]).T, axis=0, keepdims=True)
        slot = slot_of_head(info_ref, local)
        slots[slot, :KEPT, :] = packed_ref[local, :KEPT, :]
        slots[slot, KEPT:2 * KEPT, :] = jnp.concatenate([packed_ref[local, KEPT:, :64], kept_grad], axis=1)
        slots[slot, 2 * KEPT:, :] = widen_stats(stat_block(kept_log_ref[local:local + 1, :], delta))
    for spare in IDLE:
        slots[slot_of(info_ref, spare)] = jnp.zeros((2 * KEPT + 16, 128), BF)
    for chip in range(4):
        near_ref[chip] = slots[2 * chip]
        far_ref[chip] = slots[2 * chip + 1]


def local_forward(info_ref, qkv_ref, out_t_ref, log_ref, att_t_ref):
    log_ref[LOCAL_HEADS:, :] = jnp.zeros((8 - LOCAL_HEADS, ROWS), F32)
    for local in range(LOCAL_HEADS):
        scores = dot_nt(qkv_ref[1, :, span(local)], qkv_ref[0, :, span(local)] * BF(SCALE))
        peak = jnp.max(scores, axis=0, keepdims=True)
        powers = jnp.exp(scores - peak)
        total = jnp.sum(powers, axis=0, keepdims=True)
        out_t = dot_tn(qkv_ref[2, :, span(local)], powers.astype(BF)) / total
        log_row = peak + jnp.log(total)
        out_t_ref[span(local), :] = out_t
        log_ref[local:local + 1, :] = log_row
        head = head_of(info_ref[0], local)
        is_kept = jnp.bitwise_and(iota((1, ROWS), 1), 7) == jnp.bitwise_and(head, 7)
        att_t_ref[span(local), :] = jnp.where(is_kept, 0.0, out_t).astype(BF)


def widen_stats(block):
    if block.shape[1] < 128:
        block = jnp.concatenate([block, jnp.zeros((8, 128 - block.shape[1]), F32)], axis=1)
    return jnp.concatenate([block, jnp.zeros((8, 128), F32)], axis=0).astype(BF)


def local_backward(pair, info_ref, qkv_ref, grad_ref, log_ref, out_t_ref, dq_ref, dk_ref, dv_ref):
    dq_t, dk, dv = [], [], []
    for local in (2 * pair, 2 * pair + 1):
        query = qkv_ref[0, :, span(local)] * BF(SCALE)
        key = qkv_ref[1, :, span(local)]
        grad = grad_ref[:, span(local)]
        head = head_of(info_ref[0], local)
        is_kept = jnp.bitwise_and(iota((1, ROWS), 1), 7) == jnp.bitwise_and(head, 7)
        log_row = jnp.where(is_kept, MASKED, log_ref[local:local + 1, :])
        probability = jnp.exp(dot_nt(key, query) - log_row)
        delta = jnp.sum(grad.astype(F32).T * out_t_ref[span(local), :], axis=0, keepdims=True)
        score_grad = probability * (dot_nt(qkv_ref[2, :, span(local)], grad) - delta)
        score_grad = score_grad.astype(BF)
        dv.append(dot_nn(probability.astype(BF), grad))
        dk.append(dot_nn(score_grad, query))
        dq_t.append(dot_tn(key, score_grad))
    dq_ref[...] = jnp.concatenate(dq_t, axis=0).T * SCALE
    dk_ref[...] = jnp.concatenate(dk, axis=1)
    dv_ref[...] = jnp.concatenate(dv, axis=1)


def set_stats(query, key, value, grad):
    scores = dot_nt(key, query)
    peak = jnp.max(scores, axis=0, keepdims=True)
    powers = jnp.exp(scores - peak)
    total = jnp.sum(powers, axis=0, keepdims=True)
    prob_grad = dot_nt(value, grad)
    delta = jnp.sum(powers * prob_grad, axis=0, keepdims=True) / total
    return scores, prob_grad, powers, total, peak + jnp.log(total), delta


def merge(old_log, old_delta, new_log, new_delta):
    joint = log_add(old_log, new_log)
    return joint, jnp.exp(old_log - joint) * old_delta + jnp.exp(new_log - joint) * new_delta


def first_set(block_ref):
    joined = block_ref[:, :KEPT, :].reshape(ROWS, 128)
    other = block_ref[:, KEPT:2 * KEPT, :].reshape(ROWS, 128)
    return joined[:, :64], joined[:, 64:], other[:, :64], other[:, 64:]


def later_set(block_ref):
    joined = block_ref[:, :128, :].reshape(ROWS, 128)
    other = block_ref[:, 128:256, :].reshape(ROWS, 128)
    return joined[:, :64], joined[:, 64:], other[:, :64], other[:, 64:]


def later_stats(block_ref):
    return stat_rows(jnp.concatenate([block_ref[i, 256:264, :].astype(F32) for i in range(4)], axis=1))


def level_one(block_ref, payload_ref, stat_ref, out_t_ref):
    query, key, value, grad = first_set(block_ref)
    stats = jnp.concatenate([block_ref[i, 128:136, :KEPT].astype(F32) for i in range(8)], axis=1)
    old_log, old_delta = stat_rows(stats)
    _, _, powers, total, new_log, new_delta = set_stats(query, key, value, grad)
    joint, delta = merge(old_log, old_delta, new_log, new_delta)
    out_t_ref[...] = dot_tn(value, powers.astype(BF)) * (jnp.exp(new_log - joint) / total)
    stat_ref[0:1, :] = joint
    stat_ref[1:2, :] = delta
    stat_ref[2:, :] = jnp.zeros((6, ROWS), F32)
    payload_ref[:128, :] = block_ref[:, :16, :].reshape(128, 128)
    payload_ref[128:256, :] = block_ref[:, KEPT:KEPT + 16, :].reshape(128, 128)
    picked = dot_nt(stat_block(joint, delta).astype(BF), subset_pick(6, 4))
    payload_ref[256:, :] = widen_stats(picked)


def level_two(block_ref, payload_ref, stat_ref, out_t_ref):
    pick = subset_pick(4, 2)
    query, key, value, grad = later_set(block_ref)
    old_log, old_delta = later_stats(block_ref)
    _, _, powers, total, new_log, new_delta = set_stats(query, key, value, grad)
    joint, delta = merge(old_log, old_delta, new_log, new_delta)
    weight = (jnp.exp(new_log - joint) / total)[:, :128]
    out_t_ref[...] = dot_tn(value, powers[:, :128].astype(BF)) * weight
    stat_ref[0:1, :] = joint
    stat_ref[1:2, :] = delta
    stat_ref[2:, :] = jnp.zeros((6, ROWS), F32)
    payload_ref[:128, :] = dot_nn(pick, block_ref[:, :128, :].reshape(ROWS, 128)).astype(BF)
    payload_ref[128:256, :] = dot_nn(pick, block_ref[:, 128:256, :].reshape(ROWS, 128)).astype(BF)
    picked = dot_nt(stat_block(joint, delta).astype(BF), pick)
    payload_ref[256:, :] = widen_stats(picked)


def weigh(query, key, value, grad, log_row, delta_row):
    probability = jnp.exp(dot_nt(key, query) - log_row)
    score_grad = probability * (dot_nt(value, grad) - delta_row)
    return probability.astype(BF), score_grad.astype(BF)


def key_side(probability, score_grad, query, grad):
    return jnp.concatenate([dot_nn(score_grad, query), dot_nn(probability, grad)], axis=1)


def runs(lanes, wide, narrow):
    return jnp.bitwise_and(iota((1, lanes), 1), wide - 1) < narrow


def level_one_back(block_ref, stat_ref, dq_ref, dkv_ref):
    query, key, value, grad = first_set(block_ref)
    log_row = jnp.where(runs(ROWS, 64, 16), MASKED, stat_ref[0:1, :])
    probability, score_grad = weigh(query, key, value, grad, log_row, stat_ref[1:2, :])
    dq_ref[...] = dot_tn(key, score_grad) * SCALE
    dkv_ref[...] = key_side(probability, score_grad, query, grad)


def level_two_back(first_ref, second_ref, stat_ref, dkv1_ref, dkv1_out_ref, dkv2_ref, dq_ref):
    _, key1, value1, _ = first_set(first_ref)
    query, key, value, grad = later_set(second_ref)
    log_row = jnp.where(runs(ROWS, 16, 4), MASKED, stat_ref[0:1, :])
    delta_row = stat_ref[1:2, :]
    own_query, own_grad = query[:128], grad[:128]
    probability, score_grad = weigh(own_query, key1, value1, own_grad, log_row[:, :128], delta_row[:, :128])
    dkv1_out_ref[...] = dkv1_ref[...] + key_side(probability, score_grad, own_query, own_grad)
    dq = dot_tn(key1, score_grad)
    probability, score_grad = weigh(query, key, value, grad, log_row, delta_row)
    dkv2_ref[...] = key_side(probability[:128], score_grad[:128], query, grad)
    dq_ref[...] = (dq + dot_tn(key, score_grad[:, :128])) * SCALE


def spread_lanes(value, pick):
    high, low = split2(value)
    return dot_nn(high, pick) + dot_nn(low, pick)


def spread_stats(log_row, delta_row, pick):
    return stat_rows(dot_nn(stat_block(log_row, delta_row).astype(BF), pick))


def level_three(first_ref, second_ref, third_ref, stat1_ref, stat2_ref, out1_ref, out2_ref, dq1_ref, dkv1_ref,
                dq2_ref, dkv2_ref, near_ref, far_ref):
    pick2 = subset_pick(6, 4)
    own_lane = iota((1, 128), 1) < 32

    query, key, value, grad = later_set(third_ref)
    old_log, old_delta = later_stats(third_ref)
    scores, prob_grad, powers, total, new_log, new_delta = set_stats(query, key, value, grad)
    log3, delta3 = merge(old_log, old_delta, new_log, new_delta)
    weight = (jnp.exp(new_log - log3) / total)[:, :128]
    out3 = dot_tn(value, powers[:, :128].astype(BF)) * weight
    own_query, own_grad = query[:128], grad[:128]
    own_log, own_delta = log3[:, :128], delta3[:, :128]

    _, key1, value1, _ = first_set(first_ref)
    octet_log = jnp.where(own_lane, own_log, MASKED)
    probability, score_grad = weigh(own_query, key1, value1, own_grad, octet_log, own_delta)
    dkv1 = dkv1_ref[...] + key_side(probability, score_grad, own_query, own_grad)
    dq = dot_tn(key1, score_grad)
    _, key2, value2, _ = later_set(second_ref)
    probability, score_grad = weigh(own_query, key2, value2, own_grad, own_log, own_delta)
    dkv2 = dkv2_ref[...] + key_side(probability[:128], score_grad[:128], own_query, own_grad)
    dq = dq + dot_tn(key2, score_grad)
    probability = jnp.exp(scores[:, :128] - own_log)
    dq = dq + dot_tn(key, (probability * (prob_grad[:, :128] - own_delta)).astype(BF))
    probability = jnp.exp(scores[:32] - log3)
    score_grad = (probability * (prob_grad[:32] - delta3)).astype(BF)
    dkv3 = key_side(probability.astype(BF), score_grad, query, grad)

    place = iota((128, 1), 0)
    target = lax.shift_left(lax.shift_right_logical(place, 2), 4) + jnp.bitwise_and(place, 3)
    own_pick = one_hot((iota((128, 128), 1) == target) & (place < 32))
    spread_log, spread_delta = spread_stats(own_log, own_delta, own_pick)
    in_third = runs(128, 16, 4)
    log2 = jnp.where(in_third, spread_log, stat2_ref[0:1, :128])
    delta2 = jnp.where(in_third, spread_delta, stat2_ref[1:2, :128])
    merged_t = jnp.where(own_lane, jnp.concatenate([dq * SCALE, out3], axis=0), 0.0)
    fade2 = jnp.exp(stat2_ref[0:1, :128] - log2)
    base_t = jnp.concatenate([dq2_ref[...], out2_ref[...] * fade2], axis=0)
    merged_t = base_t + spread_lanes(merged_t, own_pick)
    high, low = split2(dkv3)
    dkv2 = dkv2 + dot_tn(own_pick[:32], high) + dot_tn(own_pick[:32], low)

    spread_log, spread_delta = spread_stats(log2, delta2, pick2)
    in_second = runs(ROWS, 64, 16)
    log1 = jnp.where(in_second, spread_log, stat1_ref[0:1, :])
    delta1 = jnp.where(in_second, spread_delta, stat1_ref[1:2, :])
    fade1 = jnp.exp(stat1_ref[0:1, :] - log1)
    base_t = jnp.concatenate([dq1_ref[...], out1_ref[...] * fade1], axis=0)
    merged_t = base_t + spread_lanes(merged_t, pick2)
    high, low = split2(dkv2)
    dkv1 = dkv1 + dot_tn(pick2, high) + dot_tn(pick2, low)

    rows = merged_t.T.astype(BF)
    dkv1 = dkv1.astype(BF)
    stats = stat_block(log1, delta1)
    for slot in range(8):
        part = slice(slot * KEPT, (slot + 1) * KEPT)
        target_ref = far_ref if slot % 2 else near_ref
        target_ref[slot // 2, :KEPT, :] = rows[part]
        target_ref[slot // 2, KEPT:2 * KEPT, :] = dkv1[part]
        target_ref[slot // 2, 2 * KEPT:, :] = widen_stats(stats[:, part])


def returned_stats(block):
    return stat_rows(block[2 * KEPT:2 * KEPT + 8, :KEPT])


def kept_attended(info_ref, back_ref, kept_out_ref, kept_log_ref, att_ref):
    for local in range(LOCAL_HEADS):
        block = back_ref[slot_of_head(info_ref, local)]
        log_total, _ = returned_stats(block)
        fade = jnp.exp(kept_log_ref[local:local + 1, :] - log_total)
        fade = jnp.broadcast_to(fade, (HEAD_DIM, KEPT)).T
        sparse = block[:KEPT, 64:].astype(F32)
        att_ref[:, span(local)] = (kept_out_ref[:, span(local)] * fade + sparse).astype(BF)


def tall_pair(half, pair):
    return jnp.concatenate([tall_pick(head_of(half, 2 * pair)), tall_pick(head_of(half, 2 * pair + 1))], axis=1)


def final_grads(info_ref, qkv_ref, packed_ref, kept_grad_ref, back_ref, tall_ref, *rest):
    early, (dq_out_ref, dk_out_ref, dv_out_ref, held, sems) = rest[:9], rest[9:]
    moves = []
    for pair in range(PAIRS):
        back = [back_ref[slot_of_head(info_ref, 2 * pair + spot)] for spot in range(2)]
        key = qkv_ref[1, :, cols(pair)]
        query = diagonal(packed_ref[2 * pair, :KEPT, :64], packed_ref[2 * pair + 1, :KEPT, :64])
        grad = diagonal(kept_grad_ref[:, span(2 * pair)], kept_grad_ref[:, span(2 * pair + 1)])
        stats = [returned_stats(block) for block in back]
        log_total = jnp.concatenate([stat[0] for stat in stats], axis=1)
        delta = jnp.concatenate([stat[1] for stat in stats], axis=1)
        tall = tall_ref[:, cols(pair)]
        probability = jnp.exp(dot_nt(key, query) - log_total)
        score_grad = (probability * (dot_nt(qkv_ref[2, :, cols(pair)], grad) - delta)).astype(BF)
        more_dk = diagonal(*(block[KEPT:2 * KEPT, :64] for block in back))
        more_dv = diagonal(*(block[KEPT:2 * KEPT, 64:] for block in back))
        dk = dot_nn(jnp.concatenate([score_grad, tall], axis=1), jnp.concatenate([query, more_dk], axis=0))
        dv = dot_nn(
            jnp.concatenate([probability.astype(BF), tall], axis=1), jnp.concatenate([grad, more_dv], axis=0)
        )
        crossed = dot_tn(score_grad, key) * SCALE
        more_dq = diagonal(
            crossed[:64, :64] + back[0][:KEPT, :64].astype(F32), crossed[64:, 64:] + back[1][:KEPT, :64].astype(F32)
        )
        dq = dot_nn(jnp.concatenate([tall, tall], axis=1), jnp.concatenate(split2(more_dq), axis=0))
        for which, (more, target) in enumerate(((dq, dq_out_ref), (dk, dk_out_ref), (dv, dv_out_ref))):
            held[pair, which] = (early[3 * pair + which][...] + more).astype(BF)
            move = pltpu.make_async_copy(held.at[pair, which], target.at[:, cols(pair)], sems.at[pair, which])
            move.start()
            moves.append(move)
    for move in moves:
        move.wait()


def mix_base(info_ref, own_att_ref, other_att_ref, own_w_ref, other_w_ref, base_ref, own_tall_ref, other_tall_ref):
    base_ref[...] = dot_tn(own_att_ref[...], own_w_ref[...]) + dot_tn(other_att_ref[...], other_w_ref[...])
    for pair in range(PAIRS):
        own_tall_ref[:, cols(pair)] = tall_pair(info_ref[0], pair)
        other_tall_ref[:, cols(pair)] = tall_pair(1 - info_ref[0], pair)


def spread_kept(tall_ref, kept_ref):
    return jnp.concatenate(
        [
            dot_nn(
                tall_ref[:, cols(pair)], diagonal(kept_ref[:, span(2 * pair)], kept_ref[:, span(2 * pair + 1)])
            ).astype(BF)
            for pair in range(PAIRS)
        ],
        axis=1,
    )


def mix_own(base_ref, kept_ref, tall_ref, w_ref, out_ref):
    out_ref[...] = base_ref[...] + dot_nn(spread_kept(tall_ref, kept_ref), w_ref[...])


def mix_other(base_ref, kept_ref, tall_ref, w_ref, out_ref, held, sems):
    rows = spread_kept(tall_ref, kept_ref)
    moves = []
    for pair in range(PAIRS):
        held[pair] = (base_ref[:, cols(pair)] + dot_nn(rows, w_ref[:, cols(pair)])).astype(BF)
        move = pltpu.make_async_copy(held.at[pair], out_ref.at[:, cols(pair)], sems.at[pair])
        move.start()
        moves.append(move)
    for move in moves:
        move.wait()


def call(kernel, outs, args, flops=0, info=None, after=(), scratch=(), far_out=False):
    shapes = tuple(jax.ShapeDtypeStruct(*out) for out in outs)
    moved = sum(a.size * a.dtype.itemsize for a in args) + sum(
        int(np.prod(shape)) * jnp.dtype(dtype).itemsize for shape, dtype in outs
    )
    scalars = () if info is None else (info,)
    last = len(scalars) + len(args)

    def run(*refs):
        kernel(*refs[:last], *refs[last + len(after):])

    name = getattr(kernel, "func", kernel).__name__
    run.__name__ = name
    near, far = pl.BlockSpec(memory_space=pltpu.VMEM), pl.BlockSpec(memory_space=pltpu.HBM)
    return pl.pallas_call(
        run,
        out_shape=shapes,
        in_specs=[pl.BlockSpec(memory_space=pltpu.SMEM)] * len(scalars)
        + [near] * len(args)
        + [pl.BlockSpec(memory_space=pl.ANY)] * len(after),
        out_specs=(far if far_out else near,) * len(outs),
        scratch_shapes=list(scratch),
        compiler_params=pltpu.CompilerParams(vmem_limit_bytes=VMEM_LIMIT),
        cost_estimate=pl.CostEstimate(flops=flops, bytes_accessed=moved, transcendentals=0),
        name=name,
    )(*scalars, *args, *after)


def partner(array):
    return lax.ppermute(array, "head", [(0, 1), (1, 0)])


def flip(array, mask):
    return lax.ppermute(array, "seq", [(i, i ^ mask) for i in range(lax.axis_size("seq"))])


def gather_pair(array, first, second):
    return jnp.stack([array, flip(array, first), flip(array, second), flip(array, first ^ second)])


def octet_exchange(near, far, order):
    crossed = flip(far, 1)
    blocks = [jnp.stack([near[chip], crossed[chip]]) for chip in range(4)]
    arrived = {chip: flip(blocks[chip], 2 * chip) for chip in order}
    return jnp.concatenate([blocks[0]] + [arrived[chip] for chip in (1, 2, 3)]), blocks[3], arrived[order[0]]


def body(queries, keys, values, weight_out, cotangent):
    half = lax.axis_index("head")
    place = lax.axis_index("seq")
    info = jnp.stack([half, jnp.bitwise_xor(place % 8, 6 * (place // 8 % 2))]).astype(jnp.int32)

    block = ((4, 2 * KEPT + 16, 128), BF)
    later_block = ((272, 128), BF)
    stat = ((8, ROWS), F32)
    square = ((ROWS, WIDE), F32)

    other_cot = partner(cotangent)
    qkv = jnp.stack([queries, keys, values])
    packed, hots = call(
        pack_data, [((LOCAL_HEADS, 2 * KEPT, 128), BF), ((WIDE, ROWS), BF)], (qkv,), flops=200000000, info=info
    )
    kept_out, kept_log = call(
        kept_forward, [((KEPT, WIDE), F32), ((8, KEPT), F32)], (qkv, packed), flops=100000000
    )
    out_t, log0, att_t = call(
        local_forward, [((WIDE, ROWS), F32), stat, ((WIDE, ROWS), BF)], (qkv,), flops=400000000, info=info,
    )
    grad, kept_grad, near, far = call(
        pack_grads, [((ROWS, WIDE), BF), ((KEPT, WIDE), BF), block, block],
        (packed, cotangent, other_cot, weight_out, hots, kept_out, kept_log), flops=400000000, info=info, after=(att_t,),
        scratch=[pltpu.VMEM((8, 2 * KEPT + 16, 128), BF)],
    )
    block1, _, arrived = octet_exchange(near, far, (3, 2, 1))
    late_w, _ = lax.optimization_barrier((weight_out, near))
    late_att, _ = lax.optimization_barrier((att_t, arrived))
    own_w = lax.dynamic_slice_in_dim(late_w, half * WIDE, WIDE, 1)
    mix_w = partner(lax.dynamic_slice_in_dim(late_w, (1 - half) * WIDE, WIDE, 1))
    other_att_t = partner(late_att)

    half_rows = ((128, 128), F32)

    def backward(pair, after):
        return call(
            functools.partial(local_backward, pair), [((ROWS, 128), F32)] * 3, (qkv, grad, log0, out_t),
            flops=300000000, info=info, after=(after,),
        )

    sent2, stat1, out1 = call(
        level_one, [later_block, stat, ((64, ROWS), F32)], (block1,), flops=100000000
    )
    block2 = gather_pair(sent2, 16, 14)
    dq1, dkv1 = call(level_one_back, [((64, ROWS), F32), ((ROWS, 128), F32)], (block1, stat1), flops=100000000)
    early = list(backward(0, sent2))
    sent3, stat2, out2 = call(
        level_two, [later_block, stat, ((64, 128), F32)], (block2,), flops=100000000,
        after=(other_att_t, mix_w, dq1, early[-1]),
    )
    block3 = gather_pair(sent3, 64, 48)
    early.extend(backward(1, sent3))
    dkv1, dkv2, dq2 = call(
        level_two_back, [((ROWS, 128), F32), half_rows, ((64, 128), F32)], (block1, block2, stat2, dkv1),
        flops=100000000,
    )
    base, own_tall, other_tall = call(
        mix_base, [square, ((ROWS, WIDE), BF), ((ROWS, WIDE), BF)],
        (late_att, other_att_t, own_w, mix_w), flops=300000000, info=info,
    )
    near, far = call(
        level_three, [block, block],
        (block1, block2, block3, stat1, stat2, out1, out2, dq1, dkv1, dq2, dkv2), flops=300000000, after=(base, early[-1]),
    )
    back, crossed, _ = octet_exchange(near, far, (2, 3, 1))
    early.extend(backward(2, crossed))
    (own_kept,) = call(
        kept_attended, [((KEPT, WIDE), BF)], (back, kept_out, kept_log), flops=10000000, info=info, after=(early[-1],)
    )
    other_kept = partner(own_kept)
    query_grad, key_grad, value_grad = call(
        final_grads, [((ROWS, WIDE), BF)] * 3, (qkv, packed, kept_grad, back, own_tall, *early),
        flops=200000000, info=info,
        scratch=[pltpu.VMEM((PAIRS, 3, ROWS, 128), BF), pltpu.SemaphoreType.DMA((PAIRS, 3))], far_out=True,
    )
    (nearly,) = call(mix_own, [square], (base, own_kept, own_tall, own_w), flops=200000000)
    (mixed,) = call(
        mix_other, [((ROWS, WIDE), BF)], (nearly, other_kept, other_tall, mix_w), flops=200000000,
        scratch=[pltpu.VMEM((PAIRS, ROWS, 128), BF), pltpu.SemaphoreType.DMA((PAIRS,))], far_out=True,
    )
    return mixed, query_grad, key_grad, value_grad


def solution(mesh):
    specs = P("seq", "head")
    return jax.shard_map(
        body,
        mesh=mesh,
        in_specs=(specs, specs, specs, P("head", None), specs),
        out_specs=(specs, specs, specs, specs),
        check_vma=False,
    )
```
